32 devices in a mesh: tm: 2 (over x), height: 16 (over z, y, core).
Axes of the slice: x: 2, y: 2, z: 4, core: 2. Of those that a mesh axis runs over, the one named last changes fastest.
Arguments:
- features: bfloat16 [96, 8, 64, 128], P(None, 'tm', 'height'), may hold values from -6 to 6
- first_gain: float32 [96], replicated, may hold values from 0.1 to 1.9
- first_weight: bfloat16 [96, 2592], replicated, may hold values from -0.125 to 0.125
- first_bias: float32 [96], replicated, may hold values from -3 to 3
- second_gain: float32 [96], replicated, may hold values from 0.1 to 1.9
- second_weight: bfloat16 [96, 2592], replicated, may hold values from -0.125 to 0.125
- second_bias: float32 [96], replicated, may hold values from -3 to 3
Outputs:
- encoded: bfloat16 [96, 8, 64, 128], P(None, 'tm', 'height')
The draws below stay inside these ranges and needn't reach their ends.
All inputs are finite; a program needn't handle non-finite values.
Results may differ from the reference program's by a relative error of at most 0.0036.
Values may be sent and summed in bfloat16 or wider, within the bound.
A program may use at most 64 MiB of HBM per device.

```python
import jax
import jax.numpy as jnp
from jax import lax

C = 96
COLS = 128
FRAMES = 8
ROWS = 64


def block_scale(stream_key, shape, pieces, smallest, top_value):
    level = 1.0
    for position, shards_of in pieces:
        steps = jax.random.uniform(jax.random.fold_in(jax.random.fold_in(stream_key, 6), position), (shards_of,), jnp.float32, smallest / len(pieces), top_value / len(pieces))
        level = level * jnp.repeat(jnp.exp(steps), shape[position] // shards_of).reshape((-1,) + (1,) * (len(shape) - 1 - position))
    return level


def scatter_about(stream_key, shape, deviation, limit, shards=(), dtype=jnp.bfloat16):
    level = block_scale(stream_key, shape, shards, -0.22, 0.18) if shards else 1.0
    drawn = jax.random.normal(stream_key, shape, jnp.float32) * deviation * level
    return jnp.minimum(jnp.maximum(drawn, -limit), limit).astype(dtype)


def setup_inputs(seed: int = 0) -> dict:
    key_list = jax.random.split(jax.random.key(seed), 8)
    return {
        "features": scatter_about(key_list[0], (C, FRAMES, ROWS, COLS), 1.0, 6.0, ((1, 2), (2, 16))),
        "first_gain": jnp.clip(1.0 + 0.18 * jax.random.normal(key_list[1], (C,), jnp.float32), 0.1, 1.9),
        "first_weight": scatter_about(key_list[2], (C, 27 * C), (27 * C) ** -0.5, 0.125),
        "first_bias": scatter_about(key_list[3], (C,), 0.5, 3.0, (), jnp.float32),
        "second_gain": jnp.clip(1.0 + 0.18 * jax.random.normal(key_list[4], (C,), jnp.float32), 0.1, 1.9),
        "second_weight": scatter_about(key_list[5], (C, 27 * C), (27 * C) ** -0.5, 0.125),
        "second_bias": scatter_about(key_list[6], (C,), 0.5, 3.0, (), jnp.float32),
    }


def activate(values, gain_vector):
    mean_square = lax.optimization_barrier(jnp.mean(values * values, axis=0, keepdims=True))
    scaled = values * lax.rsqrt(mean_square + 1e-06) * gain_vector[:, None, None, None]
    return jax.nn.silu(scaled).astype(jnp.bfloat16)

def causal_conv(inputs, weight, bias_vector):
    kernel = weight.astype(jnp.float32).reshape(C, 3, 3, 3, C).transpose(0, 4, 1, 2, 3)
    result = lax.conv_general_dilated(inputs.astype(jnp.float32)[None], kernel, (1, 1, 1), ((2, 0), (1, 1), (1, 1)), dimension_numbers=('NCDHW', 'OIDHW', 'NCDHW'), precision=lax.Precision.HIGHEST)[0]
    return result + bias_vector.astype(jnp.float32)[:, None, None, None]

def reference(features, first_gain, first_weight, first_bias, second_gain, second_weight, second_bias):
    first_act = activate(features.astype(jnp.float32), first_gain)
    hidden = causal_conv(first_act, first_weight, first_bias)
    second_act = activate(hidden, second_gain)
    branch = causal_conv(second_act, second_weight, second_bias)
    return (features.astype(jnp.float32) + branch).astype(jnp.bfloat16)
```

```python
import functools

import jax
import jax.numpy as jnp
from jax import lax
from jax.experimental import pallas as pl
from jax.experimental.pallas import tpu as pltpu
from jax.sharding import PartitionSpec as P

MESH = pl.DeviceIdType.MESH
ROW_PAIRS = ((1, 2), (0, 3))


def activate(values, gain):
    mean_square = jnp.mean(values * values, axis=0, keepdims=True)
    scaled = values * lax.rsqrt(mean_square + 1e-06) * gain
    return scaled / (1.0 + jnp.exp(-scaled))


def spread(taps, frame, row, values):
    lanes = lax.broadcasted_iota(jnp.int32, values.shape, 1)
    last = values.shape[1] - 1
    before = jnp.where(lanes == 0, 0.0, pltpu.roll(values, 1, 1))
    after = jnp.where(lanes == last, 0.0, pltpu.roll(values, last, 1))
    taps[frame, row, 0] = before.astype(jnp.bfloat16)
    taps[frame, row, 1] = values.astype(jnp.bfloat16)
    taps[frame, row, 2] = after.astype(jnp.bfloat16)


def add_frame(total, taps, weights, frame, pair):
    channels = taps.shape[3]
    columns = taps.shape[4]
    reached = [(tap, frame + 2 - tap) for tap in range(3) if 0 <= frame + 2 - tap < 4]
    low = reached[0][0] * channels
    right = jnp.concatenate(
        [taps[frame + 2, r : r + 3].reshape(9 * channels, columns) for r in pair], axis=1
    )
    part = jnp.dot(
        weights[low : low + len(reached) * channels, :],
        right,
        preferred_element_type=jnp.float32,
    )
    for i, (_, target) in enumerate(reached):
        for j, r in enumerate(pair):
            total[target, r] += part[
                i * channels : (i + 1) * channels, j * columns : (j + 1) * columns
            ]


def kernel(
    tm_count,
    height_count,
    features,
    vectors,
    first_weight,
    second_weight,
    out,
    weights_a,
    weights_b,
    own,
    above,
    below,
    earlier,
    earlier_above,
    earlier_below,
    taps_a,
    taps_b,
    total,
    send_sem,
    recv_sem,
):
    t = lax.axis_index("tm")
    h = lax.axis_index("height")
    has_prev, has_next = t > 0, t < tm_count - 1
    has_up, has_down = h > 0, h < height_count - 1
    up, down = (t, h - 1), (t, h + 1)
    later = (t + 1, h)

    barrier = pltpu.get_barrier_semaphore()
    neighbours = (
        (has_prev, (t - 1, h)),
        (has_next, later),
        (has_up, up),
        (has_down, down),
    )
    for present, device in neighbours:

        @pl.when(present)
        def _():
            pl.semaphore_signal(barrier, inc=1, device_id=device, device_id_type=MESH)

    def message(layer, slot, source, target, device):
        return pltpu.make_async_remote_copy(
            src_ref=source,
            dst_ref=target,
            send_sem=send_sem.at[layer, slot],
            recv_sem=recv_sem.at[layer, slot],
            device_id=device,
            device_id_type=MESH,
        )

    def to_up(layer, half):
        frames = pl.ds(2 * half, 2)
        return message(
            layer, half, own.at[layer, frames, 0], below.at[layer, frames], up
        )

    def to_down(layer, half):
        frames = pl.ds(2 * half, 2)
        return message(
            layer, 2 + half, own.at[layer, frames, 3], above.at[layer, frames], down
        )

    def to_later(layer, part):
        row, count = ((0, 1), (3, 1), (1, 2))[part]
        rows = pl.ds(row, count)
        return message(
            layer,
            4 + part,
            own.at[layer, pl.ds(2, 2), rows],
            earlier.at[layer, :, rows],
            later,
        )

    def pass_up(layer):
        return message(layer, 7, earlier.at[layer, :, 0], earlier_below.at[layer], up)

    def pass_down(layer):
        return message(layer, 8, earlier.at[layer, :, 3], earlier_above.at[layer], down)

    def send_rows(layer, half):
        @pl.when(has_up)
        def _():
            to_up(layer, half).start()

        @pl.when(has_down)
        def _():
            to_down(layer, half).start()

    def send_later(layer):
        @pl.when(has_next)
        def _():
            for part in range(3):
                to_later(layer, part).start()

    def clear(taps, frames, row):
        for frame in frames:
            taps[frame, row] = jnp.zeros(taps.shape[2:], taps.dtype)

    def take_rows(layer, taps, half):
        frames = range(2 * half, 2 * half + 2)

        @pl.when(has_up)
        def _():
            to_down(layer, half).wait_recv()
            for f in frames:
                spread(taps, f + 2, 0, above[layer, f].astype(jnp.float32))

        @pl.when(has_down)
        def _():
            to_up(layer, half).wait_recv()
            for f in frames:
                spread(taps, f + 2, 5, below[layer, f].astype(jnp.float32))

    def clear_edges(taps):
        @pl.when(jnp.logical_not(has_up))
        def _():
            clear(taps, range(6), 0)

        @pl.when(jnp.logical_not(has_down))
        def _():
            clear(taps, range(6), 5)

    def pass_on(layer):
        @pl.when(has_prev)
        def _():
            to_later(layer, 0).wait_recv()

            @pl.when(has_up)
            def _():
                pass_up(layer).start()

            to_later(layer, 1).wait_recv()

            @pl.when(has_down)
            def _():
                pass_down(layer).start()

    def add_earlier(layer, taps, weights):
        @pl.when(has_prev)
        def _():
            for r in (0, 3):
                for f in range(2):
                    spread(taps, f, r + 1, earlier[layer, f, r].astype(jnp.float32))
            to_later(layer, 2).wait_recv()
            for r in (1, 2):
                for f in range(2):
                    spread(taps, f, r + 1, earlier[layer, f, r].astype(jnp.float32))
            for f in (-2, -1):
                add_frame(total, taps, weights, f, ROW_PAIRS[0])

            @pl.when(has_up)
            def _():
                pass_down(layer).wait_recv()
                for f in range(2):
                    spread(taps, f, 0, earlier_above[layer, f].astype(jnp.float32))

            @pl.when(has_down)
            def _():
                pass_up(layer).wait_recv()
                for f in range(2):
                    spread(taps, f, 5, earlier_below[layer, f].astype(jnp.float32))

            for f in (-2, -1):
                add_frame(total, taps, weights, f, ROW_PAIRS[1])

    def start_total(bias):
        for f in range(4):
            for r in range(4):
                total[f, r] = jnp.broadcast_to(bias, total.shape[2:])

    gain = vectors[:, 0:1]
    for f in (2, 3, 0, 1):
        for r in range(4):
            act = activate(features[f, r].astype(jnp.float32), gain)
            own[0, f, r] = act.astype(jnp.bfloat16)
            spread(taps_a, f + 2, r + 1, act)

    pl.semaphore_wait(
        barrier,
        sum(present.astype(jnp.int32) for present, _ in neighbours),
    )
    send_rows(0, 1)
    send_rows(0, 0)
    send_later(0)

    width = first_weight.shape[1] // 3
    rows = first_weight.shape[0]
    for p in range(3):
        weights_a[p * rows : (p + 1) * rows, :] = first_weight[:, p * width : (p + 1) * width]
    for p in range(3):
        weights_b[p * rows : (p + 1) * rows, :] = second_weight[:, p * width : (p + 1) * width]

    start_total(vectors[:, 1:2])
    clear_edges(taps_a)
    clear_edges(taps_b)
    for f in range(4):
        add_frame(total, taps_a, weights_a, f, ROW_PAIRS[0])
    take_rows(0, taps_a, 1)
    take_rows(0, taps_a, 0)
    for f in range(4):
        add_frame(total, taps_a, weights_a, f, ROW_PAIRS[1])
    pass_on(0)

    gain = vectors[:, 2:3]

    def second_activation(frames):
        for f in frames:
            for r in range(4):
                act = activate(total[f, r], gain)
                own[1, f, r] = act.astype(jnp.bfloat16)
                spread(taps_b, f + 2, r + 1, act)

    second_activation((2, 3))
    send_later(1)
    send_rows(1, 1)
    add_earlier(0, taps_a, weights_a)
    second_activation((0, 1))
    send_rows(1, 0)

    start_total(vectors[:, 3:4])
    for f in range(4):
        add_frame(total, taps_b, weights_b, f, ROW_PAIRS[0])
    take_rows(1, taps_b, 1)
    take_rows(1, taps_b, 0)
    pass_on(1)
    for f in range(4):
        add_frame(total, taps_b, weights_b, f, ROW_PAIRS[1])

    def finish(frames):
        for f in frames:
            for r in range(4):
                out[f, r] = (features[f, r].astype(jnp.float32) + total[f, r]).astype(
                    jnp.bfloat16
                )

    finish((2, 3))
    add_earlier(1, taps_b, weights_b)
    finish((0, 1))

    for layer in range(2):

        @pl.when(has_up)
        def _():
            for half in range(2):
                to_up(layer, half).wait_send()

        @pl.when(has_down)
        def _():
            for half in range(2):
                to_down(layer, half).wait_send()

        @pl.when(has_next)
        def _():
            for part in range(3):
                to_later(layer, part).wait_send()

        @pl.when(has_prev & has_up)
        def _():
            pass_up(layer).wait_send()

        @pl.when(has_prev & has_down)
        def _():
            pass_down(layer).wait_send()


def local(features, first_gain, first_weight, first_bias, second_gain, second_weight, second_bias):
    channels, frames, rows, columns = features.shape
    by_row = jnp.transpose(features, (1, 2, 0, 3))
    vectors = jnp.stack([first_gain, first_bias, second_gain, second_bias], axis=1)
    vmem = pl.BlockSpec(memory_space=pltpu.VMEM)
    act = jnp.bfloat16
    stacked = (3 * channels, first_weight.shape[1] // 3)
    cells = 2 * channels * first_weight.shape[1] * frames * rows * columns
    result = pl.pallas_call(
        functools.partial(kernel, lax.axis_size("tm"), lax.axis_size("height")),
        out_shape=jax.ShapeDtypeStruct(by_row.shape, jnp.bfloat16),
        in_specs=[vmem] * 4,
        out_specs=vmem,
        scratch_shapes=[
            pltpu.VMEM(stacked, act),
            pltpu.VMEM(stacked, act),
            pltpu.VMEM((2, frames, rows, channels, columns), act),
            pltpu.VMEM((2, frames, channels, columns), act),
            pltpu.VMEM((2, frames, channels, columns), act),
            pltpu.VMEM((2, 2, rows, channels, columns), act),
            pltpu.VMEM((2, 2, channels, columns), act),
            pltpu.VMEM((2, 2, channels, columns), act),
            pltpu.VMEM((frames + 2, rows + 2, 3, channels, columns), act),
            pltpu.VMEM((frames + 2, rows + 2, 3, channels, columns), act),
            pltpu.VMEM((frames, rows, channels, columns), jnp.float32),
            pltpu.SemaphoreType.DMA((2, 9)),
            pltpu.SemaphoreType.DMA((2, 9)),
        ],
        compiler_params=pltpu.CompilerParams(
            collective_id=0, has_side_effects=True, vmem_limit_bytes=48 * 1024 * 1024
        ),
        cost_estimate=pl.CostEstimate(
            flops=2 * cells, bytes_accessed=3 * features.size * 2, transcendentals=features.size * 4
        ),
    )(by_row, vectors, first_weight, second_weight)
    return jnp.transpose(result, (2, 0, 1, 3))


def solution(mesh):
    return jax.shard_map(
        local,
        mesh=mesh,
        in_specs=(P(None, "tm", "height", None), P(), P(), P(), P(), P(), P()),
        out_specs=P(None, "tm", "height", None),
        check_vma=False,
    )
```

```python
import functools

import jax
import jax.numpy as jnp
from jax import lax
from jax.experimental import pallas as pl
from jax.experimental.pallas import tpu as pltpu
from jax.sharding import PartitionSpec as P

MESH = pl.DeviceIdType.MESH
ROW_PAIRS = ((1, 2), (0, 3))


def activate(values, gain):
    mean_square = jnp.mean(values * values, axis=0, keepdims=True)
    scaled = values * lax.rsqrt(mean_square + 1e-06) * gain
    return scaled / (1.0 + jnp.exp(-scaled))


def spread(taps, frame, row, values):
    lanes = lax.broadcasted_iota(jnp.int32, values.shape, 1)
    last = values.shape[1] - 1
    before = jnp.where(lanes == 0, 0.0, pltpu.roll(values, 1, 1))
    after = jnp.where(lanes == last, 0.0, pltpu.roll(values, last, 1))
    taps[frame, row, 0] = before.astype(jnp.bfloat16)
    taps[frame, row, 1] = values.astype(jnp.bfloat16)
    taps[frame, row, 2] = after.astype(jnp.bfloat16)


def add_frame(total, taps, weights, frame, pair):
    channels = taps.shape[3]
    columns = taps.shape[4]
    reached = [(tap, frame + 2 - tap) for tap in range(3) if 0 <= frame + 2 - tap < 4]
    low = reached[0][0] * channels
    right = jnp.concatenate(
        [taps[frame + 2, r : r + 3].reshape(9 * channels, columns) for r in pair], axis=1
    )
    part = jnp.dot(
        weights[low : low + len(reached) * channels, :],
        right,
        preferred_element_type=jnp.float32,
    )
    for i, (_, target) in enumerate(reached):
        for j, r in enumerate(pair):
            total[target, r] += part[
                i * channels : (i + 1) * channels, j * columns : (j + 1) * columns
            ]


def column(vectors, i, columns):
    wide = jnp.broadcast_to(vectors[i], (columns, vectors.shape[2]))
    return jnp.transpose(wide)


def kernel(
    tm_count,
    height_count,
    features_hbm,
    first_weight_hbm,
    second_weight_hbm,
    first_gain_hbm,
    first_bias_hbm,
    second_gain_hbm,
    second_bias_hbm,
    out,
    features,
    vectors,
    first_weight,
    second_weight,
    cells,
    weights_a,
    weights_b,
    own,
    above,
    below,
    earlier,
    earlier_above,
    earlier_below,
    taps_a,
    taps_b,
    total,
    send_sem,
    recv_sem,
    load_sem,
):
    loads = [
        pltpu.make_async_copy(source, target, load_sem.at[i])
        for i, (source, target) in enumerate(
            (
                (features_hbm, features),
                (first_gain_hbm, vectors.at[0]),
                (first_bias_hbm, vectors.at[1]),
                (second_gain_hbm, vectors.at[2]),
                (second_bias_hbm, vectors.at[3]),
                (first_weight_hbm, first_weight),
                (second_weight_hbm, second_weight),
            )
        )
    ]
    for load in loads:
        load.start()
    t = lax.axis_index("tm")
    h = lax.axis_index("height")
    has_prev, has_next = t > 0, t < tm_count - 1
    has_up, has_down = h > 0, h < height_count - 1
    up, down = (t, h - 1), (t, h + 1)
    later = (t + 1, h)

    barrier = pltpu.get_barrier_semaphore()
    neighbours = (
        (has_prev, (t - 1, h)),
        (has_next, later),
        (has_up, up),
        (has_down, down),
    )
    for present, device in neighbours:

        @pl.when(present)
        def _():
            pl.semaphore_signal(barrier, inc=1, device_id=device, device_id_type=MESH)

    def message(layer, slot, source, target, device):
        return pltpu.make_async_remote_copy(
            src_ref=source,
            dst_ref=target,
            send_sem=send_sem.at[layer, slot],
            recv_sem=recv_sem.at[layer, slot],
            device_id=device,
            device_id_type=MESH,
        )

    def to_up(layer, half):
        frames = pl.ds(2 * half, 2)
        return message(
            layer, half, own.at[layer, frames, 0], below.at[layer, frames], up
        )

    def to_down(layer, half):
        frames = pl.ds(2 * half, 2)
        return message(
            layer, 2 + half, own.at[layer, frames, 3], above.at[layer, frames], down
        )

    def to_later(layer, part):
        row, count = ((0, 1), (3, 1), (1, 2))[part]
        rows = pl.ds(row, count)
        return message(
            layer,
            4 + part,
            own.at[layer, pl.ds(2, 2), rows],
            earlier.at[layer, :, rows],
            later,
        )

    def pass_up(layer):
        return message(layer, 7, earlier.at[layer, :, 0], earlier_below.at[layer], up)

    def pass_down(layer):
        return message(layer, 8, earlier.at[layer, :, 3], earlier_above.at[layer], down)

    def send_rows(layer, half):
        @pl.when(has_up)
        def _():
            to_up(layer, half).start()

        @pl.when(has_down)
        def _():
            to_down(layer, half).start()

    def send_later(layer):
        @pl.when(has_next)
        def _():
            for part in range(3):
                to_later(layer, part).start()

    def clear(taps, frames, row):
        for frame in frames:
            taps[frame, row] = jnp.zeros(taps.shape[2:], taps.dtype)

    def take_rows(layer, taps, half):
        frames = range(2 * half, 2 * half + 2)

        @pl.when(has_up)
        def _():
            to_down(layer, half).wait_recv()
            for f in frames:
                spread(taps, f + 2, 0, above[layer, f].astype(jnp.float32))

        @pl.when(has_down)
        def _():
            to_up(layer, half).wait_recv()
            for f in frames:
                spread(taps, f + 2, 5, below[layer, f].astype(jnp.float32))

    def clear_edges(taps):
        @pl.when(jnp.logical_not(has_up))
        def _():
            clear(taps, range(6), 0)

        @pl.when(jnp.logical_not(has_down))
        def _():
            clear(taps, range(6), 5)

    def pass_on(layer):
        @pl.when(has_prev)
        def _():
            to_later(layer, 0).wait_recv()

            @pl.when(has_up)
            def _():
                pass_up(layer).start()

            to_later(layer, 1).wait_recv()

            @pl.when(has_down)
            def _():
                pass_down(layer).start()

    def add_earlier(layer, taps, weights):
        @pl.when(has_prev)
        def _():
            for r in (0, 3):
                for f in range(2):
                    spread(taps, f, r + 1, earlier[layer, f, r].astype(jnp.float32))
            to_later(layer, 2).wait_recv()
            for r in (1, 2):
                for f in range(2):
                    spread(taps, f, r + 1, earlier[layer, f, r].astype(jnp.float32))
            for f in (-2, -1):
                add_frame(total.at[layer], taps, weights, f, ROW_PAIRS[0])

            @pl.when(has_up)
            def _():
                pass_down(layer).wait_recv()
                for f in range(2):
                    spread(taps, f, 0, earlier_above[layer, f].astype(jnp.float32))

            @pl.when(has_down)
            def _():
                pass_up(layer).wait_recv()
                for f in range(2):
                    spread(taps, f, 5, earlier_below[layer, f].astype(jnp.float32))

            for f in (-2, -1):
                add_frame(total.at[layer], taps, weights, f, ROW_PAIRS[1])

    def start_total(layer, bias):
        for f in range(4):
            for r in range(4):
                total[layer, f, r] = bias

    def add_own(layer, taps, weights, frames, pair):
        for f in frames:
            add_frame(total.at[layer], taps, weights, f, ROW_PAIRS[pair])

    def feature_row(f, r):
        return cells[f, pl.ds(r, channels, stride=4), :]

    channels, columns = total.shape[3:]
    for load in loads[1:5]:
        load.wait()
    first_gain, first_bias, second_gain, second_bias = (
        column(vectors, i, columns) for i in range(4)
    )

    loads[0].wait()
    for f in range(4):
        cells[f] = features[:, f].astype(jnp.float32).reshape(4 * channels, columns)
    for f in (2, 3, 0, 1):
        for r in range(4):
            act = activate(feature_row(f, r), first_gain)
            own[0, f, r] = act.astype(jnp.bfloat16)
            spread(taps_a, f + 2, r + 1, act)

    pl.semaphore_wait(
        barrier,
        sum(present.astype(jnp.int32) for present, _ in neighbours),
    )
    send_rows(0, 1)
    send_rows(0, 0)
    send_later(0)

    def stack(weights, source):
        width = source.shape[1] // 3
        for p in range(3):
            weights[p * channels : (p + 1) * channels, :] = source[:, p * width : (p + 1) * width]

    loads[5].wait()
    stack(weights_a, first_weight)
    start_total(0, first_bias)
    clear_edges(taps_a)
    add_own(0, taps_a, weights_a, range(4), 0)
    take_rows(0, taps_a, 1)
    take_rows(0, taps_a, 0)
    add_own(0, taps_a, weights_a, range(4), 1)

    def second_activation(frames):
        for f in frames:
            for r in range(4):
                act = activate(total[0, f, r], second_gain)
                own[1, f, r] = act.astype(jnp.bfloat16)
                spread(taps_b, f + 2, r + 1, act)

    def finish(frames):
        for f in frames:
            for r in range(4):
                out[f, r] = (feature_row(f, r) + total[1, f, r]).astype(jnp.bfloat16)

    second_activation((2, 3))
    send_later(1)
    send_rows(1, 1)
    pass_on(0)

    loads[6].wait()
    stack(weights_b, second_weight)
    start_total(1, second_bias)
    clear_edges(taps_b)
    add_own(1, taps_b, weights_b, (2, 3), 0)
    take_rows(1, taps_b, 1)
    add_own(1, taps_b, weights_b, (2, 3), 1)

    add_earlier(0, taps_a, weights_a)
    second_activation((0, 1))
    send_rows(1, 0)
    add_own(1, taps_b, weights_b, (0, 1), 0)
    pass_on(1)
    take_rows(1, taps_b, 0)
    add_own(1, taps_b, weights_b, (0, 1), 1)
    finish((2, 3))
    add_earlier(1, taps_b, weights_b)
    finish((0, 1))

    for layer in range(2):

        @pl.when(has_up)
        def _():
            for half in range(2):
                to_up(layer, half).wait_send()

        @pl.when(has_down)
        def _():
            for half in range(2):
                to_down(layer, half).wait_send()

        @pl.when(has_next)
        def _():
            for part in range(3):
                to_later(layer, part).wait_send()

        @pl.when(has_prev & has_up)
        def _():
            pass_up(layer).wait_send()

        @pl.when(has_prev & has_down)
        def _():
            pass_down(layer).wait_send()


def local(features, first_gain, first_weight, first_bias, second_gain, second_weight, second_bias):
    channels, frames, rows, columns = features.shape
    vectors = [v.reshape(1, channels) for v in (first_gain, first_bias, second_gain, second_bias)]
    vmem = pl.BlockSpec(memory_space=pltpu.VMEM)
    act = jnp.bfloat16
    stacked = (3 * channels, first_weight.shape[1] // 3)
    cells = 2 * channels * first_weight.shape[1] * frames * rows * columns
    result = pl.pallas_call(
        functools.partial(kernel, lax.axis_size("tm"), lax.axis_size("height")),
        out_shape=jax.ShapeDtypeStruct((frames, rows, channels, columns), jnp.bfloat16),
        in_specs=[pl.BlockSpec(memory_space=pl.ANY)] * 7,
        out_specs=vmem,
        scratch_shapes=[
            pltpu.VMEM(features.shape, act),
            pltpu.VMEM((4, 1, channels), jnp.float32),
            pltpu.VMEM(first_weight.shape, act),
            pltpu.VMEM(second_weight.shape, act),
            pltpu.VMEM((frames, rows * channels, columns), jnp.float32),
            pltpu.VMEM(stacked, act),
            pltpu.VMEM(stacked, act),
            pltpu.VMEM((2, frames, rows, channels, columns), act),
            pltpu.VMEM((2, frames, channels, columns), act),
            pltpu.VMEM((2, frames, channels, columns), act),
            pltpu.VMEM((2, 2, rows, channels, columns), act),
            pltpu.VMEM((2, 2, channels, columns), act),
            pltpu.VMEM((2, 2, channels, columns), act),
            pltpu.VMEM((frames + 2, rows + 2, 3, channels, columns), act),
            pltpu.VMEM((frames + 2, rows + 2, 3, channels, columns), act),
            pltpu.VMEM((2, frames, rows, channels, columns), jnp.float32),
            pltpu.SemaphoreType.DMA((2, 9)),
            pltpu.SemaphoreType.DMA((2, 9)),
            pltpu.SemaphoreType.DMA((7,)),
        ],
        compiler_params=pltpu.CompilerParams(
            collective_id=0, has_side_effects=True, vmem_limit_bytes=56 * 1024 * 1024
        ),
        cost_estimate=pl.CostEstimate(
            flops=2 * cells, bytes_accessed=3 * features.size * 2, transcendentals=features.size * 4
        ),
    )(features, first_weight, second_weight, *vectors)
    return jnp.transpose(result, (2, 0, 1, 3))


def solution(mesh):
    return jax.shard_map(
        local,
        mesh=mesh,
        in_specs=(P(None, "tm", "height", None), P(), P(), P(), P(), P(), P()),
        out_specs=P(None, "tm", "height", None),
        check_vma=False,
    )
```

```python
import functools

import jax
import jax.numpy as jnp
from jax import lax
from jax.experimental import pallas as pl
from jax.experimental.pallas import tpu as pltpu
from jax.sharding import PartitionSpec as P

MESH = pl.DeviceIdType.MESH
ROW_PAIRS = ((1, 2), (0, 3))


def activate(values, gain):
    mean_square = jnp.mean(values * values, axis=0, keepdims=True)
    scaled = values * lax.rsqrt(mean_square + 1e-06) * gain
    return scaled * (0.5 + 0.5 * jnp.tanh(0.5 * scaled))


def spread(taps, frame, row, values):
    values = values.astype(jnp.bfloat16)
    lanes = lax.broadcasted_iota(jnp.int32, values.shape, 1)
    last = values.shape[1] - 1
    zero = jnp.zeros_like(values)
    taps[frame, row, 0] = jnp.where(lanes == 0, zero, pltpu.roll(values, 1, 1))
    taps[frame, row, 1] = values
    taps[frame, row, 2] = jnp.where(lanes == last, zero, pltpu.roll(values, last, 1))


def add_frame(total, taps, weights, frame, pair, targets=range(4)):
    channels = taps.shape[3]
    columns = taps.shape[4]
    reached = [(tap, frame + 2 - tap) for tap in range(3) if frame + 2 - tap in targets]
    low = reached[0][0] * channels
    right = jnp.concatenate(
        [taps[frame + 2, r : r + 3].reshape(9 * channels, columns) for r in pair], axis=1
    )
    part = jnp.dot(
        weights[low : low + len(reached) * channels, :],
        right,
        preferred_element_type=jnp.float32,
    )
    for i, (_, target) in enumerate(reached):
        for j, r in enumerate(pair):
            total[target, r] += part[
                i * channels : (i + 1) * channels, j * columns : (j + 1) * columns
            ]


def column(vectors, i, columns):
    wide = jnp.broadcast_to(vectors[i], (columns, vectors.shape[2]))
    return jnp.transpose(wide)


def kernel(
    tm_count,
    height_count,
    features_hbm,
    first_weight_hbm,
    second_weight_hbm,
    first_gain_hbm,
    first_bias_hbm,
    second_gain_hbm,
    second_bias_hbm,
    out,
    features,
    vectors,
    first_weight,
    second_weight,
    cells,
    weights_a,
    weights_b,
    own,
    above,
    below,
    earlier,
    earlier_above,
    earlier_below,
    taps_a,
    taps_b,
    total,
    send_sem,
    recv_sem,
    load_sem,
):
    loads = [
        pltpu.make_async_copy(source, target, load_sem.at[i])
        for i, (source, target) in enumerate(
            (
                (features_hbm, features),
                (first_gain_hbm, vectors.at[0]),
                (first_bias_hbm, vectors.at[1]),
                (second_gain_hbm, vectors.at[2]),
                (second_bias_hbm, vectors.at[3]),
                (first_weight_hbm, first_weight),
                (second_weight_hbm, second_weight),
            )
        )
    ]
    for load in loads:
        load.start()
    t = lax.axis_index("tm")
    h = lax.axis_index("height")
    has_prev, has_next = t > 0, t < tm_count - 1
    has_up, has_down = h > 0, h < height_count - 1
    up, down = (t, h - 1), (t, h + 1)
    later = (t + 1, h)

    barrier = pltpu.get_barrier_semaphore()
    neighbours = (
        (has_prev, (t - 1, h)),
        (has_next, later),
        (has_up, up),
        (has_down, down),
    )
    for present, device in neighbours:

        @pl.when(present)
        def _():
            pl.semaphore_signal(barrier, inc=1, device_id=device, device_id_type=MESH)

    def message(layer, slot, source, target, device):
        return pltpu.make_async_remote_copy(
            src_ref=source,
            dst_ref=target,
            send_sem=send_sem.at[layer, slot],
            recv_sem=recv_sem.at[layer, slot],
            device_id=device,
            device_id_type=MESH,
        )

    def to_up(layer, half):
        frames = pl.ds(2 * half, 2)
        return message(
            layer, half, own.at[layer, frames, 0], below.at[layer, frames], up
        )

    def to_down(layer, half):
        frames = pl.ds(2 * half, 2)
        return message(
            layer, 2 + half, own.at[layer, frames, 3], above.at[layer, frames], down
        )

    def to_later(layer, part):
        row, count = ((0, 1), (3, 1), (1, 2))[part]
        rows = pl.ds(row, count)
        return message(
            layer,
            4 + part,
            own.at[layer, pl.ds(2, 2), rows],
            earlier.at[layer, :, rows],
            later,
        )

    def pass_up(layer):
        return message(layer, 7, earlier.at[layer, :, 0], earlier_below.at[layer], up)

    def pass_down(layer):
        return message(layer, 8, earlier.at[layer, :, 3], earlier_above.at[layer], down)

    def send_rows(layer, half):
        @pl.when(has_up)
        def _():
            to_up(layer, half).start()

        @pl.when(has_down)
        def _():
            to_down(layer, half).start()

    def send_later(layer, parts):
        @pl.when(has_next)
        def _():
            for part in parts:
                to_later(layer, part).start()

    def clear(taps, frames, row):
        for frame in frames:
            taps[frame, row] = jnp.zeros(taps.shape[2:], taps.dtype)

    def take_rows(layer, taps, half):
        frames = range(2 * half, 2 * half + 2)

        @pl.when(has_up)
        def _():
            to_down(layer, half).wait_recv()
            for f in frames:
                spread(taps, f + 2, 0, above[layer, f].astype(jnp.float32))

        @pl.when(has_down)
        def _():
            to_up(layer, half).wait_recv()
            for f in frames:
                spread(taps, f + 2, 5, below[layer, f].astype(jnp.float32))

    def clear_edges(taps):
        @pl.when(jnp.logical_not(has_up))
        def _():
            clear(taps, range(6), 0)

        @pl.when(jnp.logical_not(has_down))
        def _():
            clear(taps, range(6), 5)

    def pass_on(layer):
        @pl.when(has_prev)
        def _():
            to_later(layer, 0).wait_recv()

            @pl.when(has_up)
            def _():
                pass_up(layer).start()

            to_later(layer, 1).wait_recv()

            @pl.when(has_down)
            def _():
                pass_down(layer).start()

    def add_earlier(layer, taps, weights):
        @pl.when(has_prev)
        def _():
            to_later(layer, 2).wait_recv()
            for r in range(4):
                for f in range(2):
                    spread(taps, f, r + 1, earlier[layer, f, r].astype(jnp.float32))
            for f in (-2, -1):
                add_frame(total.at[layer], taps, weights, f, ROW_PAIRS[0])

            @pl.when(has_up)
            def _():
                pass_down(layer).wait_recv()
                for f in range(2):
                    spread(taps, f, 0, earlier_above[layer, f].astype(jnp.float32))

            @pl.when(has_down)
            def _():
                pass_up(layer).wait_recv()
                for f in range(2):
                    spread(taps, f, 5, earlier_below[layer, f].astype(jnp.float32))

            for f in (-2, -1):
                add_frame(total.at[layer], taps, weights, f, ROW_PAIRS[1])

    def start_total(layer, bias):
        for f in range(4):
            for r in range(4):
                total[layer, f, r] = bias

    def add_own(layer, taps, weights, frames, pair, targets=range(4)):
        for f in frames:
            add_frame(total.at[layer], taps, weights, f, ROW_PAIRS[pair], targets)

    def feature_row(f, r):
        return cells[f, pl.ds(r, channels, stride=4), :]

    channels, columns = total.shape[3:]
    for load in loads[1:5]:
        load.wait()
    first_gain, first_bias, second_gain, second_bias = (
        column(vectors, i, columns) for i in range(4)
    )

    loads[0].wait()
    for f in range(4):
        cells[f] = features[:, f].astype(jnp.float32).reshape(4 * channels, columns)
    for f in (2, 3, 0, 1):
        for r in range(4):
            act = activate(feature_row(f, r), first_gain)
            own[0, f, r] = act.astype(jnp.bfloat16)
            spread(taps_a, f + 2, r + 1, act)

    pl.semaphore_wait(
        barrier,
        sum(present.astype(jnp.int32) for present, _ in neighbours),
    )
    send_rows(0, 1)
    send_rows(0, 0)
    send_later(0, (0, 1, 2))

    def stack(weights, source):
        width = source.shape[1] // 3
        for p in range(3):
            weights[p * channels : (p + 1) * channels, :] = source[:, p * width : (p + 1) * width]

    loads[5].wait()
    stack(weights_a, first_weight)
    start_total(0, first_bias)
    clear_edges(taps_a)

    def second_activation(frames, rows):
        for f in frames:
            for r in rows:
                act = activate(total[0, f, r], second_gain)
                own[1, f, r] = act.astype(jnp.bfloat16)
                spread(taps_b, f + 2, r + 1, act)

    def finish(frames):
        for f in frames:
            for r in range(4):
                cells[f, pl.ds(r, channels, stride=4), :] = feature_row(f, r) + total[1, f, r]
            out[:, f] = cells[f].reshape(channels, 4, columns).astype(jnp.bfloat16)

    add_own(0, taps_a, weights_a, range(4), 0, (2, 3))
    second_activation((2, 3), (1, 2))
    send_later(1, (2,))
    take_rows(0, taps_a, 1)
    take_rows(0, taps_a, 0)
    add_own(0, taps_a, weights_a, range(4), 1, (2, 3))
    second_activation((2, 3), (0, 3))
    send_later(1, (0, 1))
    send_rows(1, 1)
    pass_on(0)
    add_own(0, taps_a, weights_a, (0, 1), 0, (0, 1))
    add_own(0, taps_a, weights_a, (0, 1), 1, (0, 1))

    loads[6].wait()
    stack(weights_b, second_weight)
    start_total(1, second_bias)
    clear_edges(taps_b)
    add_own(1, taps_b, weights_b, (2, 3), 0)
    take_rows(1, taps_b, 1)
    add_own(1, taps_b, weights_b, (2, 3), 1)

    add_earlier(0, taps_a, weights_a)
    second_activation((0, 1), range(4))
    send_rows(1, 0)
    add_own(1, taps_b, weights_b, (0, 1), 0)
    pass_on(1)
    take_rows(1, taps_b, 0)
    add_own(1, taps_b, weights_b, (0, 1), 1)
    finish((2, 3))
    add_earlier(1, taps_b, weights_b)
    finish((0, 1))

    for layer in range(2):

        @pl.when(has_up)
        def _():
            for half in range(2):
                to_up(layer, half).wait_send()

        @pl.when(has_down)
        def _():
            for half in range(2):
                to_down(layer, half).wait_send()

        @pl.when(has_next)
        def _():
            for part in range(3):
                to_later(layer, part).wait_send()

        @pl.when(has_prev & has_up)
        def _():
            pass_up(layer).wait_send()

        @pl.when(has_prev & has_down)
        def _():
            pass_down(layer).wait_send()


def local(features, first_gain, first_weight, first_bias, second_gain, second_weight, second_bias):
    channels, frames, rows, columns = features.shape
    vectors = [v.reshape(1, channels) for v in (first_gain, first_bias, second_gain, second_bias)]
    vmem = pl.BlockSpec(memory_space=pltpu.VMEM)
    act = jnp.bfloat16
    stacked = (3 * channels, first_weight.shape[1] // 3)
    cells = 2 * channels * first_weight.shape[1] * frames * rows * columns
    return pl.pallas_call(
        functools.partial(kernel, lax.axis_size("tm"), lax.axis_size("height")),
        out_shape=jax.ShapeDtypeStruct(features.shape, jnp.bfloat16),
        in_specs=[pl.BlockSpec(memory_space=pltpu.HBM)] * 7,
        out_specs=vmem,
        scratch_shapes=[
            pltpu.VMEM(features.shape, act),
            pltpu.VMEM((4, 1, channels), jnp.float32),
            pltpu.VMEM(first_weight.shape, act),
            pltpu.VMEM(second_weight.shape, act),
            pltpu.VMEM((frames, rows * channels, columns), jnp.float32),
            pltpu.VMEM(stacked, act),
            pltpu.VMEM(stacked, act),
            pltpu.VMEM((2, frames, rows, channels, columns), act),
            pltpu.VMEM((2, frames, channels, columns), act),
            pltpu.VMEM((2, frames, channels, columns), act),
            pltpu.VMEM((2, 2, rows, channels, columns), act),
            pltpu.VMEM((2, 2, channels, columns), act),
            pltpu.VMEM((2, 2, channels, columns), act),
            pltpu.VMEM((frames + 2, rows + 2, 3, channels, columns), act),
            pltpu.VMEM((frames + 2, rows + 2, 3, channels, columns), act),
            pltpu.VMEM((2, frames, rows, channels, columns), jnp.float32),
            pltpu.SemaphoreType.DMA((2, 9)),
            pltpu.SemaphoreType.DMA((2, 9)),
            pltpu.SemaphoreType.DMA((7,)),
        ],
        compiler_params=pltpu.CompilerParams(
            collective_id=0, has_side_effects=True, vmem_limit_bytes=56 * 1024 * 1024
        ),
        cost_estimate=pl.CostEstimate(
            flops=2 * cells, bytes_accessed=3 * features.size * 2, transcendentals=features.size * 4
        ),
    )(features, first_weight, second_weight, *vectors)


def solution(mesh):
    return jax.shard_map(
        local,
        mesh=mesh,
        in_specs=(P(None, "tm", "height", None), P(), P(), P(), P(), P(), P()),
        out_specs=P(None, "tm", "height", None),
        check_vma=False,
    )
```

```python
import functools

import jax
import jax.numpy as jnp
from jax import lax
from jax.experimental import pallas as pl
from jax.experimental.pallas import tpu as pltpu
from jax.sharding import PartitionSpec as P

MESH = pl.DeviceIdType.MESH

def activate(values, gain):
    mean_square = jnp.mean(values * values, axis=0, keepdims=True)
    scaled = values * lax.rsqrt(mean_square + 1e-06) * gain
    return scaled * (0.5 + 0.5 * jnp.tanh(0.5 * scaled))


def spread(taps, frame, row, values):
    values = values.astype(jnp.bfloat16)
    lanes = lax.broadcasted_iota(jnp.int32, values.shape, 1)
    last = values.shape[1] - 1
    zero = jnp.zeros_like(values)
    taps[frame, row, 0] = jnp.where(lanes == 0, zero, pltpu.roll(values, 1, 1))
    taps[frame, row, 1] = values
    taps[frame, row, 2] = jnp.where(lanes == last, zero, pltpu.roll(values, last, 1))


def window(taps, frame, pair):
    shape = (9 * taps.shape[3], taps.shape[4])
    return jnp.concatenate(
        [
            jnp.concatenate([taps[frame + i, pl.ds(r, 3)].reshape(shape) for r in pair], axis=1)
            for i in range(2)
        ],
        axis=0,
    )


def multiply(weights, taps, frame, pair):
    return jnp.dot(weights, window(taps, frame, pair), preferred_element_type=jnp.float32)


def stack(weights, source):
    channels = source.shape[0]
    width = source.shape[1] // 3
    early, middle, late = (source[:, p * width : (p + 1) * width] for p in range(3))
    zero = jnp.zeros_like(early)
    for i, blocks in enumerate(((late, zero), (middle, late), (early, middle), (zero, early))):
        weights[i * channels : (i + 1) * channels, :] = jnp.concatenate(blocks, axis=1)


def column(vectors, i, columns):
    wide = jnp.broadcast_to(vectors[i], (columns, vectors.shape[2]))
    return jnp.transpose(wide)


def kernel(
    tm_count,
    height_count,
    features,
    first_weight_hbm,
    second_weight_hbm,
    first_gain_hbm,
    first_bias_hbm,
    second_gain_hbm,
    second_bias_hbm,
    out,
    vectors,
    first_weight,
    second_weight,
    weights_a,
    weights_b,
    own,
    above,
    below,
    earlier,
    earlier_above,
    earlier_below,
    taps_a,
    taps_b,
    total,
    send_sem,
    recv_sem,
    load_sem,
):
    loads = [
        pltpu.make_async_copy(source, target, load_sem.at[i])
        for i, (source, target) in enumerate(
            (
                (first_gain_hbm, vectors.at[0]),
                (first_bias_hbm, vectors.at[1]),
                (second_gain_hbm, vectors.at[2]),
                (second_bias_hbm, vectors.at[3]),
                (first_weight_hbm, first_weight),
                (second_weight_hbm, second_weight),
            )
        )
    ]
    for load in loads:
        load.start()
    t = lax.axis_index("tm")
    h = lax.axis_index("height")
    has_prev, has_next = t > 0, t < tm_count - 1
    has_up, has_down = h > 0, h < height_count - 1
    up, down = (t, h - 1), (t, h + 1)
    later = (t + 1, h)

    barrier = pltpu.get_barrier_semaphore()
    neighbours = (
        (has_prev, (t - 1, h)),
        (has_next, later),
        (has_up, up),
        (has_down, down),
    )
    for present, device in neighbours:

        @pl.when(present)
        def _():
            pl.semaphore_signal(barrier, inc=1, device_id=device, device_id_type=MESH)

    def message(layer, slot, source, target, device):
        return pltpu.make_async_remote_copy(
            src_ref=source,
            dst_ref=target,
            send_sem=send_sem.at[layer, slot],
            recv_sem=recv_sem.at[layer, slot],
            device_id=device,
            device_id_type=MESH,
        )

    def to_up(layer, half):
        frames = pl.ds(2 * half, 2)
        return message(
            layer, half, own.at[layer, frames, 0], below.at[layer, frames], up
        )

    def to_down(layer, half):
        frames = pl.ds(2 * half, 2)
        return message(
            layer, 2 + half, own.at[layer, frames, 3], above.at[layer, frames], down
        )

    def to_later(layer, part):
        row, count = ((0, 1), (3, 1), (1, 2))[part]
        rows = pl.ds(row, count)
        return message(
            layer,
            4 + part,
            own.at[layer, pl.ds(2, 2), rows],
            earlier.at[layer, :, rows],
            later,
        )

    def pass_up(layer):
        return message(layer, 7, earlier.at[layer, :, 0], earlier_below.at[layer], up)

    def pass_down(layer):
        return message(layer, 8, earlier.at[layer, :, 3], earlier_above.at[layer], down)

    def send_rows(layer, half):
        @pl.when(has_up)
        def _():
            to_up(layer, half).start()

        @pl.when(has_down)
        def _():
            to_down(layer, half).start()

    def send_later(layer, parts):
        @pl.when(has_next)
        def _():
            for part in parts:
                to_later(layer, part).start()

    def clear(taps, frames, row):
        for frame in frames:
            taps[frame, row] = jnp.zeros(taps.shape[2:], taps.dtype)

    def spread_frames(taps, first, row, source):
        def step(f, carry):
            spread(taps, first + f, row, source[f])
            return carry

        lax.fori_loop(0, 2, step, 0)

    def take_rows(layer, taps, half):
        frames = pl.ds(2 * half, 2)

        @pl.when(has_up)
        def _():
            to_down(layer, half).wait_recv()
            spread_frames(taps, 2 + 2 * half, 0, above.at[layer, frames])

        @pl.when(has_down)
        def _():
            to_up(layer, half).wait_recv()
            spread_frames(taps, 2 + 2 * half, 5, below.at[layer, frames])

    def clear_edges(taps):
        @pl.when(jnp.logical_not(has_up))
        def _():
            clear(taps, range(6), 0)

        @pl.when(jnp.logical_not(has_down))
        def _():
            clear(taps, range(6), 5)

    def pass_on(layer):
        @pl.when(has_prev)
        def _():
            to_later(layer, 0).wait_recv()

            @pl.when(has_up)
            def _():
                pass_up(layer).start()

            to_later(layer, 1).wait_recv()

            @pl.when(has_down)
            def _():
                pass_down(layer).start()

    def take_earlier(layer, taps):
        to_later(layer, 2).wait_recv()

        def step(f, carry):
            for r in range(4):
                spread(taps, f, r + 1, earlier[layer, f, r])
            return carry

        lax.fori_loop(0, 2, step, 0)

    def take_corners(layer, taps):
        @pl.when(has_up)
        def _():
            pass_down(layer).wait_recv()
            spread_frames(taps, 0, 0, earlier_above.at[layer])

        @pl.when(has_down)
        def _():
            pass_up(layer).wait_recv()
            spread_frames(taps, 0, 5, earlier_below.at[layer])

    def each_pair(step):
        def body(k, carry):
            step(k, (1 - k, 2 + k))
            return carry

        lax.fori_loop(0, 2, body, 0)

    def cut(part, i, j):
        return part[i * channels : (i + 1) * channels, j * columns : (j + 1) * columns]

    def plus_bias(part, bias):
        wide = jnp.concatenate([bias, bias], axis=1)
        return part + jnp.concatenate([wide, wide], axis=0)

    channels, columns = features.shape[2:]
    two = 2 * channels
    for load in loads[:4]:
        load.wait()
    first_gain, first_bias, second_gain, second_bias = (
        column(vectors, i, columns) for i in range(4)
    )

    def first_activation(f, carry):
        for r in range(4):
            act = activate(features[f, r].astype(jnp.float32), first_gain)
            own[0, f, r] = act.astype(jnp.bfloat16)
            spread(taps_a, f + 2, r + 1, act)
        return carry

    lax.fori_loop(0, 4, first_activation, 0)

    pl.semaphore_wait(
        barrier,
        sum(present.astype(jnp.int32) for present, _ in neighbours),
    )
    send_rows(0, 1)
    send_rows(0, 0)
    send_later(0, (0, 1, 2))

    loads[4].wait()
    stack(weights_a, first_weight)
    clear_edges(taps_a)
    clear_edges(taps_b)

    def second_activation(first, pair, part):
        for i in range(2):
            for j, r in enumerate(pair):
                act = activate(cut(part, i, j), second_gain)
                own[1, first + i, r] = act.astype(jnp.bfloat16)
                spread(taps_b, first + i + 2, r + 1, act)

    def finish(first, pair, part):
        for i in range(2):
            for j, r in enumerate(pair):
                value = features[first + i, r].astype(jnp.float32) + cut(part, i, j)
                out[first + i, r] = value.astype(jnp.bfloat16)

    def first_late(k, pair):
        @pl.when(k == 1)
        def _():
            take_rows(0, taps_a, 1)
            take_rows(0, taps_a, 0)

        part = multiply(weights_a[two:, :], taps_a, 2, pair)
        part = part + multiply(weights_a[:two, :], taps_a, 4, pair)
        second_activation(2, pair, plus_bias(part, first_bias))

        @pl.when(k == 0)
        def _():
            send_later(1, (2,))

    each_pair(first_late)
    send_later(1, (0, 1))
    send_rows(1, 1)
    pass_on(0)

    def first_early(k, pair):
        total[0, k] = plus_bias(multiply(weights_a[:two, :], taps_a, 2, pair), first_bias)

    each_pair(first_early)

    loads[5].wait()
    stack(weights_b, second_weight)

    def second_late(k, pair):
        @pl.when(k == 1)
        def _():
            take_rows(1, taps_b, 1)

        total[1, k] = plus_bias(multiply(weights_b[:two, :], taps_b, 4, pair), second_bias)

    each_pair(second_late)

    @pl.when(has_prev)
    def _():
        take_earlier(0, taps_a)

    def first_earlier(k, pair):
        @pl.when(has_prev)
        def _():
            @pl.when(k == 1)
            def _():
                take_corners(0, taps_a)

            total[0, k] += multiply(weights_a[two:, :], taps_a, 0, pair)

        second_activation(0, pair, total[0, k])

    each_pair(first_earlier)
    send_rows(1, 0)

    def second_early(k, pair):
        @pl.when(k == 1)
        def _():
            pass_on(1)
            take_rows(1, taps_b, 0)

        part = multiply(weights_b[...], taps_b, 2, pair)
        finish(2, pair, total[1, k] + part[two:, :])
        total[0, k] = plus_bias(part[:two, :], second_bias)

    each_pair(second_early)

    @pl.when(has_prev)
    def _():
        take_earlier(1, taps_b)

    def second_earlier(k, pair):
        @pl.when(has_prev)
        def _():
            @pl.when(k == 1)
            def _():
                take_corners(1, taps_b)

            total[0, k] += multiply(weights_b[two:, :], taps_b, 0, pair)

        finish(0, pair, total[0, k])

    each_pair(second_earlier)

    for layer in range(2):

        @pl.when(has_up)
        def _():
            for half in range(2):
                to_up(layer, half).wait_send()

        @pl.when(has_down)
        def _():
            for half in range(2):
                to_down(layer, half).wait_send()

        @pl.when(has_next)
        def _():
            for part in range(3):
                to_later(layer, part).wait_send()

        @pl.when(has_prev & has_up)
        def _():
            pass_up(layer).wait_send()

        @pl.when(has_prev & has_down)
        def _():
            pass_down(layer).wait_send()


def local(features, first_gain, first_weight, first_bias, second_gain, second_weight, second_bias):
    channels, frames, rows, columns = features.shape
    by_row = jnp.transpose(features, (1, 2, 0, 3))
    vectors = [v.reshape(1, channels) for v in (first_gain, first_bias, second_gain, second_bias)]
    vmem = pl.BlockSpec(memory_space=pltpu.VMEM)
    act = jnp.bfloat16
    stacked = (4 * channels, 2 * first_weight.shape[1] // 3)
    cells = 2 * channels * first_weight.shape[1] * frames * rows * columns
    result = pl.pallas_call(
        functools.partial(kernel, lax.axis_size("tm"), lax.axis_size("height")),
        out_shape=jax.ShapeDtypeStruct(by_row.shape, jnp.bfloat16),
        in_specs=[vmem] + [pl.BlockSpec(memory_space=pltpu.HBM)] * 6,
        out_specs=vmem,
        scratch_shapes=[
            pltpu.VMEM((4, 1, channels), jnp.float32),
            pltpu.VMEM(first_weight.shape, act),
            pltpu.VMEM(second_weight.shape, act),
            pltpu.VMEM(stacked, act),
            pltpu.VMEM(stacked, act),
            pltpu.VMEM((2, frames, rows, channels, columns), act),
            pltpu.VMEM((2, frames, channels, columns), act),
            pltpu.VMEM((2, frames, channels, columns), act),
            pltpu.VMEM((2, 2, rows, channels, columns), act),
            pltpu.VMEM((2, 2, channels, columns), act),
            pltpu.VMEM((2, 2, channels, columns), act),
            pltpu.VMEM((frames + 2, rows + 2, 3, channels, columns), act),
            pltpu.VMEM((frames + 2, rows + 2, 3, channels, columns), act),
            pltpu.VMEM((2, 2, 2 * channels, 2 * columns), jnp.float32),
            pltpu.SemaphoreType.DMA((2, 9)),
            pltpu.SemaphoreType.DMA((2, 9)),
            pltpu.SemaphoreType.DMA((6,)),
        ],
        compiler_params=pltpu.CompilerParams(
            collective_id=0, has_side_effects=True, vmem_limit_bytes=48 * 1024 * 1024
        ),
        cost_estimate=pl.CostEstimate(
            flops=2 * cells, bytes_accessed=3 * features.size * 2, transcendentals=features.size * 4
        ),
    )(by_row, first_weight, second_weight, *vectors)
    return jnp.transpose(result, (2, 0, 1, 3))


def solution(mesh):
    return jax.shard_map(
        local,
        mesh=mesh,
        in_specs=(P(None, "tm", "height", None), P(), P(), P(), P(), P(), P()),
        out_specs=P(None, "tm", "height", None),
        check_vma=False,
    )
```

```python
import functools

import jax
import jax.numpy as jnp
from jax import lax
from jax.experimental import pallas as pl
from jax.experimental.pallas import tpu as pltpu
from jax.sharding import PartitionSpec as P

MESH = pl.DeviceIdType.MESH

def activate(values, gain):
    mean_square = jnp.mean(values * values, axis=0, keepdims=True)
    scaled = values * lax.rsqrt(mean_square + 1e-06) * gain
    return scaled * (0.5 + 0.5 * jnp.tanh(0.5 * scaled))


def spread(taps, frame, row, values):
    values = values.astype(jnp.bfloat16)
    lanes = lax.broadcasted_iota(jnp.int32, values.shape, 1)
    last = values.shape[1] - 1
    zero = jnp.zeros_like(values)
    taps[frame, row, 0] = jnp.where(lanes == 0, zero, pltpu.roll(values, 1, 1))
    taps[frame, row, 1] = values
    taps[frame, row, 2] = jnp.where(lanes == last, zero, pltpu.roll(values, last, 1))


def padded_width(width):
    return -(-width // 128) * 128


def window(taps, frame, pair):
    width, columns = 9 * taps.shape[3], taps.shape[4]
    zero = jnp.zeros((padded_width(width) - width, len(pair) * columns), taps.dtype)
    blocks = []
    for i in range(2):
        rows = [taps[frame + i, pl.ds(r, 3)].reshape(width, columns) for r in pair]
        blocks += [jnp.concatenate(rows, axis=1), zero]
    return jnp.concatenate(blocks, axis=0)


def multiply(weights, taps, frame, pair):
    return jnp.dot(weights, window(taps, frame, pair), preferred_element_type=jnp.float32)


def stack(weights, source):
    channels = source.shape[0]
    width = source.shape[1] // 3
    full = padded_width(width)
    zero = jnp.zeros((channels, full - width), source.dtype)
    early, middle, late = (
        jnp.concatenate([source[:, p * width : (p + 1) * width], zero], axis=1) for p in range(3)
    )
    none = jnp.zeros_like(early)
    for i, blocks in enumerate(((late, none), (middle, late), (early, middle), (none, early))):
        for j, block in enumerate(blocks):
            weights[i * channels : (i + 1) * channels, j * full : (j + 1) * full] = block


def column(vectors, i, columns):
    wide = jnp.broadcast_to(vectors[i], (columns, vectors.shape[2]))
    return jnp.transpose(wide)


def kernel(
    tm_count,
    height_count,
    features,
    first_weight_hbm,
    second_weight_hbm,
    first_gain_hbm,
    first_bias_hbm,
    second_gain_hbm,
    second_bias_hbm,
    out,
    vectors,
    first_weight,
    second_weight,
    weights_a,
    weights_b,
    own,
    above,
    below,
    earlier,
    earlier_above,
    earlier_below,
    taps_a,
    taps_b,
    total,
    send_sem,
    recv_sem,
    load_sem,
):
    loads = [
        pltpu.make_async_copy(source, target, load_sem.at[i])
        for i, (source, target) in enumerate(
            (
                (first_gain_hbm, vectors.at[0]),
                (first_bias_hbm, vectors.at[1]),
                (second_gain_hbm, vectors.at[2]),
                (second_bias_hbm, vectors.at[3]),
                (first_weight_hbm, first_weight),
                (second_weight_hbm, second_weight),
            )
        )
    ]
    for load in loads:
        load.start()
    t = lax.axis_index("tm")
    h = lax.axis_index("height")
    has_prev, has_next = t > 0, t < tm_count - 1
    has_up, has_down = h > 0, h < height_count - 1
    up, down = (t, h - 1), (t, h + 1)
    later = (t + 1, h)

    barrier = pltpu.get_barrier_semaphore()
    neighbours = (
        (has_prev, (t - 1, h)),
        (has_next, later),
        (has_up, up),
        (has_down, down),
    )
    for present, device in neighbours:

        @pl.when(present)
        def _():
            pl.semaphore_signal(barrier, inc=1, device_id=device, device_id_type=MESH)

    def message(layer, slot, source, target, device):
        return pltpu.make_async_remote_copy(
            src_ref=source,
            dst_ref=target,
            send_sem=send_sem.at[layer, slot],
            recv_sem=recv_sem.at[layer, slot],
            device_id=device,
            device_id_type=MESH,
        )

    def to_up(layer, half):
        frames = pl.ds(2 * half, 2)
        return message(
            layer, half, own.at[layer, frames, 0], below.at[layer, frames], up
        )

    def to_down(layer, half):
        frames = pl.ds(2 * half, 2)
        return message(
            layer, 2 + half, own.at[layer, frames, 3], above.at[layer, frames], down
        )

    def to_later(layer, part):
        row, count = ((0, 1), (3, 1), (1, 2))[part]
        rows = pl.ds(row, count)
        return message(
            layer,
            4 + part,
            own.at[layer, pl.ds(2, 2), rows],
            earlier.at[layer, :, rows],
            later,
        )

    def pass_up(layer):
        return message(layer, 7, earlier.at[layer, :, 0], earlier_below.at[layer], up)

    def pass_down(layer):
        return message(layer, 8, earlier.at[layer, :, 3], earlier_above.at[layer], down)

    def send_rows(layer, half):
        @pl.when(has_up)
        def _():
            to_up(layer, half).start()

        @pl.when(has_down)
        def _():
            to_down(layer, half).start()

    def send_later(layer, parts):
        @pl.when(has_next)
        def _():
            for part in parts:
                to_later(layer, part).start()

    def clear(taps, frames, row):
        for frame in frames:
            taps[frame, row] = jnp.zeros(taps.shape[2:], taps.dtype)

    def spread_frames(taps, first, row, source):
        def step(f, carry):
            spread(taps, first + f, row, source[f])
            return carry

        lax.fori_loop(0, 2, step, 0)

    def take_rows(layer, taps, half):
        frames = pl.ds(2 * half, 2)

        @pl.when(has_up)
        def _():
            to_down(layer, half).wait_recv()
            spread_frames(taps, 2 + 2 * half, 0, above.at[layer, frames])

        @pl.when(has_down)
        def _():
            to_up(layer, half).wait_recv()
            spread_frames(taps, 2 + 2 * half, 5, below.at[layer, frames])

    def clear_edges(taps):
        @pl.when(jnp.logical_not(has_up))
        def _():
            clear(taps, range(6), 0)

        @pl.when(jnp.logical_not(has_down))
        def _():
            clear(taps, range(6), 5)

    def pass_on(layer):
        @pl.when(has_prev)
        def _():
            to_later(layer, 0).wait_recv()

            @pl.when(has_up)
            def _():
                pass_up(layer).start()

            to_later(layer, 1).wait_recv()

            @pl.when(has_down)
            def _():
                pass_down(layer).start()

    def take_earlier(layer, taps):
        to_later(layer, 2).wait_recv()

        def step(f, carry):
            for r in range(4):
                spread(taps, f, r + 1, earlier[layer, f, r])
            return carry

        lax.fori_loop(0, 2, step, 0)

    def take_corners(layer, taps):
        @pl.when(has_up)
        def _():
            pass_down(layer).wait_recv()
            spread_frames(taps, 0, 0, earlier_above.at[layer])

        @pl.when(has_down)
        def _():
            pass_up(layer).wait_recv()
            spread_frames(taps, 0, 5, earlier_below.at[layer])

    def each_pair(step):
        def body(k, carry):
            step(k, (1 - k, 2 + k))
            return carry

        lax.fori_loop(0, 2, body, 0)

    def cut(part, i, j):
        return part[i * channels : (i + 1) * channels, j * columns : (j + 1) * columns]

    def plus_bias(part, bias):
        wide = jnp.concatenate([bias, bias], axis=1)
        return part + jnp.concatenate([wide, wide], axis=0)

    channels, columns = features.shape[2:]
    two = 2 * channels
    for load in loads[:4]:
        load.wait()
    first_gain, first_bias, second_gain, second_bias = (
        column(vectors, i, columns) for i in range(4)
    )

    def first_activation(f, carry):
        for r in range(4):
            act = activate(features[f, r].astype(jnp.float32), first_gain)
            own[0, f, r] = act.astype(jnp.bfloat16)
            spread(taps_a, f + 2, r + 1, act)
        return carry

    lax.fori_loop(0, 4, first_activation, 0)

    pl.semaphore_wait(
        barrier,
        sum(present.astype(jnp.int32) for present, _ in neighbours),
    )
    send_rows(0, 1)
    send_rows(0, 0)
    send_later(0, (0, 1, 2))

    loads[4].wait()
    stack(weights_a, first_weight)
    clear_edges(taps_a)
    clear_edges(taps_b)

    def second_activation(first, pair, part):
        for i in range(2):
            for j, r in enumerate(pair):
                act = activate(cut(part, i, j), second_gain)
                own[1, first + i, r] = act.astype(jnp.bfloat16)
                spread(taps_b, first + i + 2, r + 1, act)

    def finish(first, pair, part):
        for i in range(2):
            for j, r in enumerate(pair):
                value = features[first + i, r].astype(jnp.float32) + cut(part, i, j)
                out[first + i, r] = value.astype(jnp.bfloat16)

    def first_late(k, pair):
        @pl.when(k == 1)
        def _():
            take_rows(0, taps_a, 1)
            take_rows(0, taps_a, 0)

        part = multiply(weights_a[two:, :], taps_a, 2, pair)
        part = part + multiply(weights_a[:two, :], taps_a, 4, pair)
        second_activation(2, pair, plus_bias(part, first_bias))

        @pl.when(k == 0)
        def _():
            send_later(1, (2,))

    each_pair(first_late)
    send_later(1, (0, 1))
    send_rows(1, 1)
    pass_on(0)

    def first_early(k, pair):
        total[0, k] = plus_bias(multiply(weights_a[:two, :], taps_a, 2, pair), first_bias)

    each_pair(first_early)

    loads[5].wait()
    stack(weights_b, second_weight)

    def second_late(k, pair):
        total[1, k] = plus_bias(multiply(weights_b[:two, :], taps_b, 4, pair), second_bias)

    second_late(0, (1, 2))

    @pl.when(has_prev)
    def _():
        take_earlier(0, taps_a)

    def first_earlier(k, pair):
        @pl.when(has_prev)
        def _():
            @pl.when(k == 1)
            def _():
                take_corners(0, taps_a)

            total[0, k] += multiply(weights_a[two:, :], taps_a, 0, pair)

        second_activation(0, pair, total[0, k])

    each_pair(first_earlier)
    send_rows(1, 0)
    take_rows(1, taps_b, 1)
    second_late(1, (0, 3))

    def second_early(k, pair):
        @pl.when(k == 1)
        def _():
            pass_on(1)
            take_rows(1, taps_b, 0)

        part = multiply(weights_b[...], taps_b, 2, pair)
        finish(2, pair, total[1, k] + part[two:, :])
        total[0, k] = plus_bias(part[:two, :], second_bias)

    each_pair(second_early)

    @pl.when(has_prev)
    def _():
        take_earlier(1, taps_b)

    def second_earlier(k, pair):
        @pl.when(has_prev)
        def _():
            @pl.when(k == 1)
            def _():
                take_corners(1, taps_b)

            total[0, k] += multiply(weights_b[two:, :], taps_b, 0, pair)

        finish(0, pair, total[0, k])

    each_pair(second_earlier)

    for layer in range(2):

        @pl.when(has_up)
        def _():
            for half in range(2):
                to_up(layer, half).wait_send()

        @pl.when(has_down)
        def _():
            for half in range(2):
                to_down(layer, half).wait_send()

        @pl.when(has_next)
        def _():
            for part in range(3):
                to_later(layer, part).wait_send()

        @pl.when(has_prev & has_up)
        def _():
            pass_up(layer).wait_send()

        @pl.when(has_prev & has_down)
        def _():
            pass_down(layer).wait_send()


def local(features, first_gain, first_weight, first_bias, second_gain, second_weight, second_bias):
    channels, frames, rows, columns = features.shape
    by_row = jnp.transpose(features, (1, 2, 0, 3))
    vectors = [v.reshape(1, channels) for v in (first_gain, first_bias, second_gain, second_bias)]
    vmem = pl.BlockSpec(memory_space=pltpu.VMEM)
    act = jnp.bfloat16
    stacked = (4 * channels, 2 * padded_width(first_weight.shape[1] // 3))
    cells = 2 * channels * first_weight.shape[1] * frames * rows * columns
    result = pl.pallas_call(
        functools.partial(kernel, lax.axis_size("tm"), lax.axis_size("height")),
        out_shape=jax.ShapeDtypeStruct(by_row.shape, jnp.bfloat16),
        in_specs=[vmem] + [pl.BlockSpec(memory_space=pltpu.HBM)] * 6,
        out_specs=vmem,
        scratch_shapes=[
            pltpu.VMEM((4, 1, channels), jnp.float32),
            pltpu.VMEM(first_weight.shape, act),
            pltpu.VMEM(second_weight.shape, act),
            pltpu.VMEM(stacked, act),
            pltpu.VMEM(stacked, act),
            pltpu.VMEM((2, frames, rows, channels, columns), act),
            pltpu.VMEM((2, frames, channels, columns), act),
            pltpu.VMEM((2, frames, channels, columns), act),
            pltpu.VMEM((2, 2, rows, channels, columns), act),
            pltpu.VMEM((2, 2, channels, columns), act),
            pltpu.VMEM((2, 2, channels, columns), act),
            pltpu.VMEM((frames + 2, rows + 2, 3, channels, columns), act),
            pltpu.VMEM((frames + 2, rows + 2, 3, channels, columns), act),
            pltpu.VMEM((2, 2, 2 * channels, 2 * columns), jnp.float32),
            pltpu.SemaphoreType.DMA((2, 9)),
            pltpu.SemaphoreType.DMA((2, 9)),
            pltpu.SemaphoreType.DMA((6,)),
        ],
        compiler_params=pltpu.CompilerParams(
            collective_id=0, has_side_effects=True, vmem_limit_bytes=53 * 1024 * 1024
        ),
        cost_estimate=pl.CostEstimate(
            flops=2 * cells, bytes_accessed=3 * features.size * 2, transcendentals=features.size * 4
        ),
    )(by_row, first_weight, second_weight, *vectors)
    return jnp.transpose(result, (2, 0, 1, 3))


def solution(mesh):
    return jax.shard_map(
        local,
        mesh=mesh,
        in_specs=(P(None, "tm", "height", None), P(), P(), P(), P(), P(), P()),
        out_specs=P(None, "tm", "height", None),
        check_vma=False,
    )
```

```python
import functools

import jax
import jax.numpy as jnp
from jax import lax
from jax.experimental import pallas as pl
from jax.experimental.pallas import tpu as pltpu
from jax.sharding import PartitionSpec as P

MESH = pl.DeviceIdType.MESH

def activate(values, gain):
    mean_square = jnp.mean(values * values, axis=0, keepdims=True)
    scaled = values * lax.rsqrt(mean_square + 1e-06) * gain
    return scaled * (0.5 + 0.5 * jnp.tanh(0.5 * scaled))


def spread(taps, frame, row, values):
    values = values.astype(jnp.bfloat16)
    lanes = lax.broadcasted_iota(jnp.int32, values.shape, 1)
    last = values.shape[1] - 1
    zero = jnp.zeros_like(values)
    taps[frame, row, 0] = jnp.where(lanes == 0, zero, pltpu.roll(values, 1, 1))
    taps[frame, row, 1] = values
    taps[frame, row, 2] = jnp.where(lanes == last, zero, pltpu.roll(values, last, 1))


def padded_width(width):
    return -(-width // 128) * 128


def window(taps, frame, pair):
    width, columns = 9 * taps.shape[3], taps.shape[4]
    zero = jnp.zeros((padded_width(width) - width, len(pair) * columns), taps.dtype)
    blocks = []
    for i in range(2):
        rows = [taps[frame + i, pl.ds(r, 3)].reshape(width, columns) for r in pair]
        blocks += [jnp.concatenate(rows, axis=1), zero]
    return jnp.concatenate(blocks, axis=0)


def multiply(weights, taps, frame, pair):
    return jnp.dot(weights, window(taps, frame, pair), preferred_element_type=jnp.float32)


def stack(weights, source):
    channels = source.shape[0]
    width = source.shape[1] // 3
    full = padded_width(width)
    zero = jnp.zeros((channels, full - width), source.dtype)
    early, middle, late = (
        jnp.concatenate([source[:, p * width : (p + 1) * width], zero], axis=1) for p in range(3)
    )
    none = jnp.zeros_like(early)
    for i, blocks in enumerate(((late, none), (middle, late), (early, middle), (none, early))):
        for j, block in enumerate(blocks):
            weights[i * channels : (i + 1) * channels, j * full : (j + 1) * full] = block


def column(vectors, i, columns):
    wide = jnp.broadcast_to(vectors[i], (columns, vectors.shape[2]))
    return jnp.transpose(wide)


def kernel(
    tm_count,
    height_count,
    features,
    first_weight_hbm,
    second_weight_hbm,
    first_gain_hbm,
    first_bias_hbm,
    second_gain_hbm,
    second_bias_hbm,
    out,
    vectors,
    first_weight,
    second_weight,
    weights_a,
    weights_b,
    own,
    above,
    below,
    earlier,
    passed,
    corners,
    taps_a,
    taps_b,
    total,
    send_sem,
    recv_sem,
    load_sem,
):
    loads = [
        pltpu.make_async_copy(source, target, load_sem.at[i])
        for i, (source, target) in enumerate(
            (
                (first_gain_hbm, vectors.at[0]),
                (first_bias_hbm, vectors.at[1]),
                (second_gain_hbm, vectors.at[2]),
                (second_bias_hbm, vectors.at[3]),
                (first_weight_hbm, first_weight),
                (second_weight_hbm, second_weight),
            )
        )
    ]
    for load in loads:
        load.start()
    t = lax.axis_index("tm")
    h = lax.axis_index("height")
    has_prev, has_next = t > 0, t < tm_count - 1
    has_up, has_down = h > 0, h < height_count - 1
    up, down = (t, h - 1), (t, h + 1)
    later = (t + 1, h)
    even = h % 2 == 0
    has_outer = (even & has_up) | (jnp.logical_not(even) & has_down)
    outer = h - 1 + 2 * (h % 2)
    has_inner_up = jnp.logical_not(even) & has_up
    has_inner_down = even & has_down

    barrier = pltpu.get_barrier_semaphore()
    neighbours = (
        (has_prev, (t - 1, h)),
        (has_next, later),
        (has_up, up),
        (has_down, down),
        (has_prev & has_outer, (t - 1, outer)),
        (has_next & has_outer, (t + 1, outer)),
    )
    for present, device in neighbours:

        @pl.when(present)
        def _():
            pl.semaphore_signal(barrier, inc=1, device_id=device, device_id_type=MESH)

    def message(layer, slot, source, target, device):
        return pltpu.make_async_remote_copy(
            src_ref=source,
            dst_ref=target,
            send_sem=send_sem.at[layer, slot],
            recv_sem=recv_sem.at[layer, slot],
            device_id=device,
            device_id_type=MESH,
        )

    def to_up(layer, half):
        frames = pl.ds(2 * half, 2)
        return message(
            layer, half, own.at[layer, frames, 0], below.at[layer, frames], up
        )

    def to_down(layer, half):
        frames = pl.ds(2 * half, 2)
        return message(
            layer, 2 + half, own.at[layer, frames, 3], above.at[layer, frames], down
        )

    def to_later(layer, part):
        row, count = ((0, 1), (3, 1), (1, 2))[part]
        rows = pl.ds(row, count)
        return message(
            layer,
            4 + part,
            own.at[layer, pl.ds(2, 2), rows],
            earlier.at[layer, :, rows],
            later,
        )

    def pass_up(layer):
        return message(layer, 7, earlier.at[layer, :, 0], passed.at[layer], up)

    def pass_down(layer):
        return message(layer, 8, earlier.at[layer, :, 3], passed.at[layer], down)

    def corner(layer):
        row = 3 * (h % 2)
        return message(
            layer,
            9,
            own.at[layer, pl.ds(2, 2), row],
            corners.at[layer],
            (t + 1, outer),
        )

    def send_rows(layer, half):
        @pl.when(has_up)
        def _():
            to_up(layer, half).start()

        @pl.when(has_down)
        def _():
            to_down(layer, half).start()

    def send_later(layer, parts):
        @pl.when(has_next)
        def _():
            for part in parts:
                to_later(layer, part).start()
                if part == 1:

                    @pl.when(has_outer)
                    def _():
                        corner(layer).start()

    def clear(taps, frames, row):
        for frame in frames:
            taps[frame, row] = jnp.zeros(taps.shape[2:], taps.dtype)

    def spread_frames(taps, first, row, source):
        def step(f, carry):
            spread(taps, first + f, row, source[f])
            return carry

        lax.fori_loop(0, 2, step, 0)

    def take_rows(layer, taps, half):
        frames = pl.ds(2 * half, 2)

        @pl.when(has_up)
        def _():
            to_down(layer, half).wait_recv()
            spread_frames(taps, 2 + 2 * half, 0, above.at[layer, frames])

        @pl.when(has_down)
        def _():
            to_up(layer, half).wait_recv()
            spread_frames(taps, 2 + 2 * half, 5, below.at[layer, frames])

    def clear_edges(taps):
        @pl.when(jnp.logical_not(has_up))
        def _():
            clear(taps, range(6), 0)

        @pl.when(jnp.logical_not(has_down))
        def _():
            clear(taps, range(6), 5)

    def pass_on(layer):
        @pl.when(has_prev)
        def _():
            to_later(layer, 0).wait_recv()

            @pl.when(has_inner_up)
            def _():
                pass_up(layer).start()

            to_later(layer, 1).wait_recv()

            @pl.when(has_inner_down)
            def _():
                pass_down(layer).start()

    def take_earlier(layer, taps, rows):
        def step(f, carry):
            for r in rows:
                spread(taps, f, r + 1, earlier[layer, f, r])
            return carry

        lax.fori_loop(0, 2, step, 0)

    def take_inner(layer, taps):
        @pl.when(has_prev)
        def _():
            to_later(layer, 2).wait_recv()
            take_earlier(layer, taps, (1, 2))

    def take_outer(layer, taps):
        @pl.when(has_prev)
        def _():
            take_earlier(layer, taps, (0, 3))

    def take_corners(layer, taps):
        @pl.when(has_inner_up)
        def _():
            pass_down(layer).wait_recv()
            spread_frames(taps, 0, 0, passed.at[layer])

        @pl.when(has_inner_down)
        def _():
            pass_up(layer).wait_recv()
            spread_frames(taps, 0, 5, passed.at[layer])

        @pl.when(has_outer)
        def _():
            corner(layer).wait_recv()
            spread_frames(taps, 0, 5 * (h % 2), corners.at[layer])

    def each_pair(step):
        def body(k, carry):
            step(k, (1 - k, 2 + k))
            return carry

        lax.fori_loop(0, 2, body, 0)

    def cut(part, i, j):
        return part[i * channels : (i + 1) * channels, j * columns : (j + 1) * columns]

    def plus_bias(part, bias):
        wide = jnp.concatenate([bias, bias], axis=1)
        return part + jnp.concatenate([wide, wide], axis=0)

    channels, columns = features.shape[2:]
    two = 2 * channels
    for load in loads[:4]:
        load.wait()
    first_gain, first_bias, second_gain, second_bias = (
        column(vectors, i, columns) for i in range(4)
    )

    def first_activation(f, carry):
        for r in range(4):
            act = activate(features[f, r].astype(jnp.float32), first_gain)
            own[0, f, r] = act.astype(jnp.bfloat16)
            spread(taps_a, f + 2, r + 1, act)
        return carry

    lax.fori_loop(0, 4, first_activation, 0)

    pl.semaphore_wait(
        barrier,
        sum(present.astype(jnp.int32) for present, _ in neighbours),
    )
    send_rows(0, 1)
    send_rows(0, 0)
    send_later(0, (0, 1, 2))

    loads[4].wait()
    stack(weights_a, first_weight)
    clear_edges(taps_a)
    clear_edges(taps_b)

    def second_activation(first, pair, part):
        for i in range(2):
            for j, r in enumerate(pair):
                act = activate(cut(part, i, j), second_gain)
                own[1, first + i, r] = act.astype(jnp.bfloat16)
                spread(taps_b, first + i + 2, r + 1, act)

    def finish(first, pair, part):
        for i in range(2):
            for j, r in enumerate(pair):
                value = features[first + i, r].astype(jnp.float32) + cut(part, i, j)
                out[first + i, r] = value.astype(jnp.bfloat16)

    def first_late(k, pair):
        @pl.when(k == 1)
        def _():
            take_rows(0, taps_a, 1)
            take_rows(0, taps_a, 0)

        part = multiply(weights_a[two:, :], taps_a, 2, pair)
        part = part + multiply(weights_a[:two, :], taps_a, 4, pair)
        second_activation(2, pair, plus_bias(part, first_bias))

        @pl.when(k == 0)
        def _():
            send_later(1, (2,))

    each_pair(first_late)
    send_later(1, (0, 1))
    send_rows(1, 1)
    pass_on(0)

    def first_early(k, pair):
        total[0, k] = plus_bias(multiply(weights_a[:two, :], taps_a, 2, pair), first_bias)

    each_pair(first_early)

    loads[5].wait()
    stack(weights_b, second_weight)

    def second_late(k, pair):
        total[1, k] = plus_bias(multiply(weights_b[:two, :], taps_b, 4, pair), second_bias)

    second_late(0, (1, 2))

    take_inner(0, taps_a)
    take_outer(0, taps_a)

    def first_earlier(k, pair):
        @pl.when(has_prev)
        def _():
            @pl.when(k == 1)
            def _():
                take_corners(0, taps_a)

            total[0, k] += multiply(weights_a[two:, :], taps_a, 0, pair)

        second_activation(0, pair, total[0, k])

    each_pair(first_earlier)
    send_rows(1, 0)
    take_rows(1, taps_b, 1)
    second_late(1, (0, 3))

    take_inner(1, taps_b)

    def second_early(k, pair):
        @pl.when(k == 1)
        def _():
            pass_on(1)
            take_rows(1, taps_b, 0)

        part = multiply(weights_b[...], taps_b, 2, pair)
        finish(2, pair, total[1, k] + part[two:, :])
        total[0, k] = plus_bias(part[:two, :], second_bias)

    each_pair(second_early)

    take_outer(1, taps_b)

    def second_earlier(k, pair):
        @pl.when(has_prev)
        def _():
            @pl.when(k == 1)
            def _():
                take_corners(1, taps_b)

            total[0, k] += multiply(weights_b[two:, :], taps_b, 0, pair)

        finish(0, pair, total[0, k])

    each_pair(second_earlier)

    for layer in range(2):

        @pl.when(has_up)
        def _():
            for half in range(2):
                to_up(layer, half).wait_send()

        @pl.when(has_down)
        def _():
            for half in range(2):
                to_down(layer, half).wait_send()

        @pl.when(has_next)
        def _():
            for part in range(3):
                to_later(layer, part).wait_send()

        @pl.when(has_next & has_outer)
        def _():
            corner(layer).wait_send()

        @pl.when(has_prev & has_inner_up)
        def _():
            pass_up(layer).wait_send()

        @pl.when(has_prev & has_inner_down)
        def _():
            pass_down(layer).wait_send()


def local(features, first_gain, first_weight, first_bias, second_gain, second_weight, second_bias):
    channels, frames, rows, columns = features.shape
    by_row = jnp.transpose(features, (1, 2, 0, 3))
    vectors = [v.reshape(1, channels) for v in (first_gain, first_bias, second_gain, second_bias)]
    vmem = pl.BlockSpec(memory_space=pltpu.VMEM)
    act = jnp.bfloat16
    stacked = (4 * channels, 2 * padded_width(first_weight.shape[1] // 3))
    cells = 2 * channels * first_weight.shape[1] * frames * rows * columns
    result = pl.pallas_call(
        functools.partial(kernel, lax.axis_size("tm"), lax.axis_size("height")),
        out_shape=jax.ShapeDtypeStruct(by_row.shape, jnp.bfloat16),
        in_specs=[vmem] + [pl.BlockSpec(memory_space=pltpu.HBM)] * 6,
        out_specs=vmem,
        scratch_shapes=[
            pltpu.VMEM((4, 1, channels), jnp.float32),
            pltpu.VMEM(first_weight.shape, act),
            pltpu.VMEM(second_weight.shape, act),
            pltpu.VMEM(stacked, act),
            pltpu.VMEM(stacked, act),
            pltpu.VMEM((2, frames, rows, channels, columns), act),
            pltpu.VMEM((2, frames, channels, columns), act),
            pltpu.VMEM((2, frames, channels, columns), act),
            pltpu.VMEM((2, 2, rows, channels, columns), act),
            pltpu.VMEM((2, 2, channels, columns), act),
            pltpu.VMEM((2, 2, channels, columns), act),
            pltpu.VMEM((frames + 2, rows + 2, 3, channels, columns), act),
            pltpu.VMEM((frames + 2, rows + 2, 3, channels, columns), act),
            pltpu.VMEM((2, 2, 2 * channels, 2 * columns), jnp.float32),
            pltpu.SemaphoreType.DMA((2, 10)),
            pltpu.SemaphoreType.DMA((2, 10)),
            pltpu.SemaphoreType.DMA((6,)),
        ],
        compiler_params=pltpu.CompilerParams(
            collective_id=0, has_side_effects=True, vmem_limit_bytes=53 * 1024 * 1024
        ),
        cost_estimate=pl.CostEstimate(
            flops=2 * cells, bytes_accessed=3 * features.size * 2, transcendentals=features.size * 4
        ),
    )(by_row, first_weight, second_weight, *vectors)
    return jnp.transpose(result, (2, 0, 1, 3))


def solution(mesh):
    return jax.shard_map(
        local,
        mesh=mesh,
        in_specs=(P(None, "tm", "height", None), P(), P(), P(), P(), P(), P()),
        out_specs=P(None, "tm", "height", None),
        check_vma=False,
    )
```

```python
import functools

import jax
import jax.numpy as jnp
from jax import lax
from jax.experimental import pallas as pl
from jax.experimental.pallas import tpu as pltpu
from jax.sharding import PartitionSpec as P

MESH = pl.DeviceIdType.MESH

def activate(values, gain):
    mean_square = jnp.mean(values * values, axis=0, keepdims=True)
    scaled = values * lax.rsqrt(mean_square + 1e-06) * gain
    return scaled * (0.5 + 0.5 * jnp.tanh(0.5 * scaled))


def spread(taps, frame, row, values):
    values = values.astype(jnp.bfloat16)
    lanes = lax.broadcasted_iota(jnp.int32, values.shape, 1)
    last = values.shape[1] - 1
    zero = jnp.zeros_like(values)
    taps[frame, row, 0] = jnp.where(lanes == 0, zero, pltpu.roll(values, 1, 1))
    taps[frame, row, 1] = values
    taps[frame, row, 2] = jnp.where(lanes == last, zero, pltpu.roll(values, last, 1))


def padded_width(width):
    return -(-width // 128) * 128


def window(taps, frame, pair):
    width, columns = 9 * taps.shape[3], taps.shape[4]
    zero = jnp.zeros((padded_width(width) - width, len(pair) * columns), taps.dtype)
    blocks = []
    for i in range(2):
        rows = [taps[frame + i, pl.ds(r, 3)].reshape(width, columns) for r in pair]
        blocks += [jnp.concatenate(rows, axis=1), zero]
    return jnp.concatenate(blocks, axis=0)


def multiply(weights, taps, frame, pair):
    return jnp.dot(weights, window(taps, frame, pair), preferred_element_type=jnp.float32)


def stack(weights, source):
    channels = source.shape[0]
    width = source.shape[1] // 3
    full = padded_width(width)
    zero = jnp.zeros((channels, full - width), source.dtype)
    early, middle, late = (
        jnp.concatenate([source[:, p * width : (p + 1) * width], zero], axis=1) for p in range(3)
    )
    none = jnp.zeros_like(early)
    for i, blocks in enumerate(((late, none), (middle, late), (early, middle), (none, early))):
        for j, block in enumerate(blocks):
            weights[i * channels : (i + 1) * channels, j * full : (j + 1) * full] = block


def column(vectors, i, columns):
    wide = jnp.broadcast_to(vectors[i], (columns, vectors.shape[2]))
    return jnp.transpose(wide)


def kernel(
    tm_count,
    height_count,
    features,
    first_weight_hbm,
    second_weight_hbm,
    first_gain_hbm,
    first_bias_hbm,
    second_gain_hbm,
    second_bias_hbm,
    out,
    vectors,
    first_weight,
    second_weight,
    weights_a,
    weights_b,
    own,
    above,
    below,
    earlier,
    earlier_above,
    earlier_below,
    partial,
    taps_a,
    taps_b,
    total,
    send_sem,
    recv_sem,
    load_sem,
):
    loads = [
        pltpu.make_async_copy(source, target, load_sem.at[i])
        for i, (source, target) in enumerate(
            (
                (first_gain_hbm, vectors.at[0]),
                (first_bias_hbm, vectors.at[1]),
                (second_gain_hbm, vectors.at[2]),
                (second_bias_hbm, vectors.at[3]),
                (first_weight_hbm, first_weight),
                (second_weight_hbm, second_weight),
            )
        )
    ]
    for load in loads:
        load.start()
    t = lax.axis_index("tm")
    h = lax.axis_index("height")
    has_prev, has_next = t > 0, t < tm_count - 1
    has_up, has_down = h > 0, h < height_count - 1
    up, down = (t, h - 1), (t, h + 1)
    later = (t + 1, h)

    barrier = pltpu.get_barrier_semaphore()
    neighbours = (
        (has_prev, (t - 1, h)),
        (has_next, later),
        (has_up, up),
        (has_down, down),
    )
    for present, device in neighbours:

        @pl.when(present)
        def _():
            pl.semaphore_signal(barrier, inc=1, device_id=device, device_id_type=MESH)

    def message(layer, slot, source, target, device):
        return pltpu.make_async_remote_copy(
            src_ref=source,
            dst_ref=target,
            send_sem=send_sem.at[layer, slot],
            recv_sem=recv_sem.at[layer, slot],
            device_id=device,
            device_id_type=MESH,
        )

    def to_up(layer, half):
        frames = pl.ds(2 * half, 2)
        return message(
            layer, half, own.at[layer, frames, 0], below.at[layer, frames], up
        )

    def to_down(layer, half):
        frames = pl.ds(2 * half, 2)
        return message(
            layer, 2 + half, own.at[layer, frames, 3], above.at[layer, frames], down
        )

    def to_later(layer, part):
        row, count = ((0, 1), (3, 1), (1, 2))[part]
        rows = pl.ds(row, count)
        return message(
            layer,
            4 + part,
            partial.at[:, rows] if layer else own.at[layer, pl.ds(2, 2), rows],
            earlier.at[layer, :, rows],
            later,
        )

    def pass_up(layer):
        return message(layer, 7, earlier.at[layer, :, 0], earlier_below.at[layer], up)

    def pass_down(layer):
        return message(layer, 8, earlier.at[layer, :, 3], earlier_above.at[layer], down)

    def send_rows(layer, half):
        @pl.when(has_up)
        def _():
            to_up(layer, half).start()

        @pl.when(has_down)
        def _():
            to_down(layer, half).start()

    def send_later(layer, parts):
        @pl.when(has_next)
        def _():
            for part in parts:
                to_later(layer, part).start()

    def clear(taps, frames, row):
        for frame in frames:
            taps[frame, row] = jnp.zeros(taps.shape[2:], taps.dtype)

    def spread_frames(taps, first, row, source):
        def step(f, carry):
            spread(taps, first + f, row, source[f])
            return carry

        lax.fori_loop(0, 2, step, 0)

    def take_rows(layer, taps, half):
        frames = pl.ds(2 * half, 2)

        @pl.when(has_up)
        def _():
            to_down(layer, half).wait_recv()
            spread_frames(taps, 2 + 2 * half, 0, above.at[layer, frames])

        @pl.when(has_down)
        def _():
            to_up(layer, half).wait_recv()
            spread_frames(taps, 2 + 2 * half, 5, below.at[layer, frames])

    def clear_edges(taps):
        @pl.when(jnp.logical_not(has_up))
        def _():
            clear(taps, range(6), 0)

        @pl.when(jnp.logical_not(has_down))
        def _():
            clear(taps, range(6), 5)

    def pass_on(layer):
        @pl.when(has_prev)
        def _():
            to_later(layer, 0).wait_recv()

            @pl.when(has_up)
            def _():
                pass_up(layer).start()

            to_later(layer, 1).wait_recv()

            @pl.when(has_down)
            def _():
                pass_down(layer).start()

    def take_earlier(layer, taps):
        to_later(layer, 2).wait_recv()

        def step(f, carry):
            for r in range(4):
                spread(taps, f, r + 1, earlier[layer, f, r])
            return carry

        lax.fori_loop(0, 2, step, 0)

    def take_corners(layer, taps):
        @pl.when(has_up)
        def _():
            pass_down(layer).wait_recv()
            spread_frames(taps, 0, 0, earlier_above.at[layer])

        @pl.when(has_down)
        def _():
            pass_up(layer).wait_recv()
            spread_frames(taps, 0, 5, earlier_below.at[layer])

    def each_pair(step):
        def body(k, carry):
            step(k, (1 - k, 2 + k))
            return carry

        lax.fori_loop(0, 2, body, 0)

    def cut(part, i, j):
        return part[i * channels : (i + 1) * channels, j * columns : (j + 1) * columns]

    def plus_bias(part, bias):
        wide = jnp.concatenate([bias, bias], axis=1)
        return part + jnp.concatenate([wide, wide], axis=0)

    channels, columns = features.shape[2:]
    two = 2 * channels
    for load in loads[:4]:
        load.wait()
    first_gain, first_bias, second_gain, second_bias = (
        column(vectors, i, columns) for i in range(4)
    )

    def first_activation(f, carry):
        for r in range(4):
            act = activate(features[f, r].astype(jnp.float32), first_gain)
            own[0, f, r] = act.astype(jnp.bfloat16)
            spread(taps_a, f + 2, r + 1, act)
        return carry

    lax.fori_loop(0, 4, first_activation, 0)

    pl.semaphore_wait(
        barrier,
        sum(present.astype(jnp.int32) for present, _ in neighbours),
    )
    send_rows(0, 1)
    send_rows(0, 0)
    send_later(0, (0, 1, 2))

    loads[4].wait()
    stack(weights_a, first_weight)
    clear_edges(taps_a)
    clear_edges(taps_b)

    def second_activation(first, pair, part):
        for i in range(2):
            for j, r in enumerate(pair):
                act = activate(cut(part, i, j), second_gain)
                own[1, first + i, r] = act.astype(jnp.bfloat16)
                spread(taps_b, first + i + 2, r + 1, act)

    def finish(first, pair, part):
        for i in range(2):
            for j, r in enumerate(pair):
                value = features[first + i, r].astype(jnp.float32) + cut(part, i, j)
                out[first + i, r] = value.astype(jnp.bfloat16)

    def first_late(k, pair):
        @pl.when(k == 1)
        def _():
            loads[5].wait()
            stack(weights_b, second_weight)
            take_rows(0, taps_a, 1)
            take_rows(0, taps_a, 0)

        part = multiply(weights_a[two:, :], taps_a, 2, pair)
        part = part + multiply(weights_a[:two, :], taps_a, 4, pair)
        second_activation(2, pair, plus_bias(part, first_bias))

    each_pair(first_late)
    send_rows(1, 1)

    def second_late(k, pair):
        @pl.when(has_next)
        def _():
            part = multiply(weights_b[...], taps_b, 4, pair)
            total[1, k] = plus_bias(part[:two, :], second_bias)
            for i in range(2):
                for j, r in enumerate(pair):
                    partial[i, r] = cut(part, 2 + i, j).astype(jnp.bfloat16)

        @pl.when(jnp.logical_not(has_next))
        def _():
            part = multiply(weights_b[:two, :], taps_b, 4, pair)
            total[1, k] = plus_bias(part, second_bias)

    second_late(0, (1, 2))
    send_later(1, (2,))

    def first_early(k, pair):
        total[0, k] = plus_bias(multiply(weights_a[:two, :], taps_a, 2, pair), first_bias)

    each_pair(first_early)

    pass_on(0)
    take_rows(1, taps_b, 1)
    second_late(1, (0, 3))
    send_later(1, (0, 1))

    @pl.when(has_prev)
    def _():
        take_earlier(0, taps_a)

    def first_earlier(k, pair):
        @pl.when(has_prev)
        def _():
            @pl.when(k == 1)
            def _():
                take_corners(0, taps_a)

            total[0, k] += multiply(weights_a[two:, :], taps_a, 0, pair)

        second_activation(0, pair, total[0, k])

    each_pair(first_earlier)
    send_rows(1, 0)

    def second_early(k, pair):
        @pl.when(k == 1)
        def _():
            take_rows(1, taps_b, 0)

        part = multiply(weights_b[...], taps_b, 2, pair)
        finish(2, pair, total[1, k] + part[two:, :])
        total[0, k] = plus_bias(part[:two, :], second_bias)

        @pl.when(has_prev)
        def _():
            @pl.when(k == 0)
            def _():
                to_later(1, 2).wait_recv()

            @pl.when(k == 1)
            def _():
                to_later(1, 0).wait_recv()
                to_later(1, 1).wait_recv()

            for i in range(2):
                for j, r in enumerate(pair):
                    block = (
                        pl.ds(i * channels, channels),
                        pl.ds(j * columns, columns),
                    )
                    total[0, k, *block] += earlier[1, i, r].astype(jnp.float32)

        finish(0, pair, total[0, k])

    each_pair(second_early)

    for layer in range(2):

        @pl.when(has_up)
        def _():
            for half in range(2):
                to_up(layer, half).wait_send()

        @pl.when(has_down)
        def _():
            for half in range(2):
                to_down(layer, half).wait_send()

        @pl.when(has_next)
        def _():
            for part in range(3):
                to_later(layer, part).wait_send()

    @pl.when(has_prev & has_up)
    def _():
        pass_up(0).wait_send()

    @pl.when(has_prev & has_down)
    def _():
        pass_down(0).wait_send()


def local(features, first_gain, first_weight, first_bias, second_gain, second_weight, second_bias):
    channels, frames, rows, columns = features.shape
    by_row = jnp.transpose(features, (1, 2, 0, 3))
    vectors = [v.reshape(1, channels) for v in (first_gain, first_bias, second_gain, second_bias)]
    vmem = pl.BlockSpec(memory_space=pltpu.VMEM)
    act = jnp.bfloat16
    stacked = (4 * channels, 2 * padded_width(first_weight.shape[1] // 3))
    cells = 2 * channels * first_weight.shape[1] * frames * rows * columns
    result = pl.pallas_call(
        functools.partial(kernel, lax.axis_size("tm"), lax.axis_size("height")),
        out_shape=jax.ShapeDtypeStruct(by_row.shape, jnp.bfloat16),
        in_specs=[vmem] + [pl.BlockSpec(memory_space=pltpu.HBM)] * 6,
        out_specs=vmem,
        scratch_shapes=[
            pltpu.VMEM((4, 1, channels), jnp.float32),
            pltpu.VMEM(first_weight.shape, act),
            pltpu.VMEM(second_weight.shape, act),
            pltpu.VMEM(stacked, act),
            pltpu.VMEM(stacked, act),
            pltpu.VMEM((2, frames, rows, channels, columns), act),
            pltpu.VMEM((2, frames, channels, columns), act),
            pltpu.VMEM((2, frames, channels, columns), act),
            pltpu.VMEM((2, 2, rows, channels, columns), act),
            pltpu.VMEM((2, 2, channels, columns), act),
            pltpu.VMEM((2, 2, channels, columns), act),
            pltpu.VMEM((2, rows, channels, columns), act),
            pltpu.VMEM((frames + 2, rows + 2, 3, channels, columns), act),
            pltpu.VMEM((frames + 2, rows + 2, 3, channels, columns), act),
            pltpu.VMEM((2, 2, 2 * channels, 2 * columns), jnp.float32),
            pltpu.SemaphoreType.DMA((2, 9)),
            pltpu.SemaphoreType.DMA((2, 9)),
            pltpu.SemaphoreType.DMA((6,)),
        ],
        compiler_params=pltpu.CompilerParams(
            collective_id=0, has_side_effects=True, vmem_limit_bytes=53 * 1024 * 1024
        ),
        cost_estimate=pl.CostEstimate(
            flops=2 * cells, bytes_accessed=3 * features.size * 2, transcendentals=features.size * 4
        ),
    )(by_row, first_weight, second_weight, *vectors)
    return jnp.transpose(result, (2, 0, 1, 3))


def solution(mesh):
    return jax.shard_map(
        local,
        mesh=mesh,
        in_specs=(P(None, "tm", "height", None), P(), P(), P(), P(), P(), P()),
        out_specs=P(None, "tm", "height", None),
        check_vma=False,
    )
```

```python
import functools

import jax
import jax.numpy as jnp
from jax import lax
from jax.experimental import pallas as pl
from jax.experimental.pallas import tpu as pltpu
from jax.sharding import PartitionSpec as P

MESH = pl.DeviceIdType.MESH

def activate(values, gain):
    mean_square = jnp.mean(values * values, axis=0, keepdims=True)
    scaled = values * lax.rsqrt(mean_square + 1e-06) * gain
    return scaled * (0.5 + 0.5 * jnp.tanh(0.5 * scaled))


def spread(taps, frame, row, values):
    values = values.astype(jnp.bfloat16)
    lanes = lax.broadcasted_iota(jnp.int32, values.shape, 1)
    last = values.shape[1] - 1
    zero = jnp.zeros_like(values)
    taps[frame, row, 0] = jnp.where(lanes == 0, zero, pltpu.roll(values, 1, 1))
    taps[frame, row, 1] = values
    taps[frame, row, 2] = jnp.where(lanes == last, zero, pltpu.roll(values, last, 1))


def padded_width(width):
    return -(-width // 128) * 128


def window(taps, frame, pair):
    width, columns = 9 * taps.shape[3], taps.shape[4]
    zero = jnp.zeros((padded_width(width) - width, len(pair) * columns), taps.dtype)
    blocks = []
    for i in range(2):
        rows = [taps[frame + i, pl.ds(r, 3)].reshape(width, columns) for r in pair]
        blocks += [jnp.concatenate(rows, axis=1), zero]
    return jnp.concatenate(blocks, axis=0)


def multiply(weights, taps, frame, pair):
    return jnp.dot(weights, window(taps, frame, pair), preferred_element_type=jnp.float32)


def stack(weights, source):
    channels = source.shape[0]
    width = source.shape[1] // 3
    full = padded_width(width)
    zero = jnp.zeros((channels, full - width), source.dtype)
    early, middle, late = (
        jnp.concatenate([source[:, p * width : (p + 1) * width], zero], axis=1) for p in range(3)
    )
    none = jnp.zeros_like(early)
    for i, blocks in enumerate(((late, none), (middle, late), (early, middle), (none, early))):
        for j, block in enumerate(blocks):
            weights[i * channels : (i + 1) * channels, j * full : (j + 1) * full] = block


def column(vectors, i, columns):
    wide = jnp.broadcast_to(vectors[i], (columns, vectors.shape[2]))
    return jnp.transpose(wide)


def kernel(
    tm_count,
    height_count,
    features,
    first_weight_hbm,
    second_weight_hbm,
    first_gain_hbm,
    first_bias_hbm,
    second_gain_hbm,
    second_bias_hbm,
    out,
    vectors,
    first_weight,
    second_weight,
    weights_a,
    weights_b,
    own,
    above,
    below,
    earlier,
    earlier_above,
    earlier_below,
    partial,
    taps_a,
    taps_b,
    total,
    send_sem,
    recv_sem,
    load_sem,
):
    loads = [
        pltpu.make_async_copy(source, target, load_sem.at[i])
        for i, (source, target) in enumerate(
            (
                (first_gain_hbm, vectors.at[0]),
                (first_bias_hbm, vectors.at[1]),
                (second_gain_hbm, vectors.at[2]),
                (second_bias_hbm, vectors.at[3]),
                (first_weight_hbm, first_weight),
                (second_weight_hbm, second_weight),
            )
        )
    ]
    for load in loads:
        load.start()
    t = lax.axis_index("tm")
    h = lax.axis_index("height")
    has_prev, has_next = t > 0, t < tm_count - 1
    has_up, has_down = h > 0, h < height_count - 1
    up, down = (t, h - 1), (t, h + 1)
    later = (t + 1, h)

    barrier = pltpu.get_barrier_semaphore()
    neighbours = (
        (has_prev, (t - 1, h)),
        (has_next, later),
        (has_up, up),
        (has_down, down),
    )
    for present, device in neighbours:

        @pl.when(present)
        def _():
            pl.semaphore_signal(barrier, inc=1, device_id=device, device_id_type=MESH)

    def message(layer, slot, source, target, device):
        return pltpu.make_async_remote_copy(
            src_ref=source,
            dst_ref=target,
            send_sem=send_sem.at[layer, slot],
            recv_sem=recv_sem.at[layer, slot],
            device_id=device,
            device_id_type=MESH,
        )

    def halves(layer):
        return range(2) if layer else range(1)

    def span(layer, half):
        return pl.ds(2 * half, 2) if layer else pl.ds(0, 4)

    def to_up(layer, half):
        frames = span(layer, half)
        return message(
            layer, half, own.at[layer, frames, 0], below.at[layer, frames], up
        )

    def to_down(layer, half):
        frames = span(layer, half)
        return message(
            layer, 2 + half, own.at[layer, frames, 3], above.at[layer, frames], down
        )

    def to_later(layer, part):
        row, count = ((0, 1), (3, 1), (1, 2))[part]
        rows = pl.ds(row, count)
        return message(
            layer,
            4 + part,
            partial.at[:, rows] if layer else own.at[layer, pl.ds(2, 2), rows],
            earlier.at[layer, :, rows],
            later,
        )

    def pass_up(layer):
        return message(layer, 7, earlier.at[layer, :, 0], earlier_below.at[layer], up)

    def pass_down(layer):
        return message(layer, 8, earlier.at[layer, :, 3], earlier_above.at[layer], down)

    def send_rows(layer, half):
        @pl.when(has_up)
        def _():
            to_up(layer, half).start()

        @pl.when(has_down)
        def _():
            to_down(layer, half).start()

    def send_later(layer, parts):
        @pl.when(has_next)
        def _():
            for part in parts:
                to_later(layer, part).start()

    def clear(taps, frames, row):
        for frame in frames:
            taps[frame, row] = jnp.zeros(taps.shape[2:], taps.dtype)

    def spread_frames(taps, first, row, source, count=2):
        def step(f, carry):
            spread(taps, first + f, row, source[f])
            return carry

        lax.fori_loop(0, count, step, 0)

    def take_rows(layer, taps, half):
        frames = span(layer, half)
        count = 2 if layer else 4

        @pl.when(has_up)
        def _():
            to_down(layer, half).wait_recv()
            spread_frames(taps, 2 + 2 * half, 0, above.at[layer, frames], count)

        @pl.when(has_down)
        def _():
            to_up(layer, half).wait_recv()
            spread_frames(taps, 2 + 2 * half, 5, below.at[layer, frames], count)

    def clear_edges(taps):
        @pl.when(jnp.logical_not(has_up))
        def _():
            clear(taps, range(6), 0)

        @pl.when(jnp.logical_not(has_down))
        def _():
            clear(taps, range(6), 5)

    def pass_on(layer):
        @pl.when(has_prev)
        def _():
            to_later(layer, 0).wait_recv()

            @pl.when(has_up)
            def _():
                pass_up(layer).start()

            to_later(layer, 1).wait_recv()

            @pl.when(has_down)
            def _():
                pass_down(layer).start()

    def take_earlier(layer, taps):
        to_later(layer, 2).wait_recv()

        def step(f, carry):
            for r in range(4):
                spread(taps, f, r + 1, earlier[layer, f, r])
            return carry

        lax.fori_loop(0, 2, step, 0)

    def take_corners(layer, taps):
        @pl.when(has_up)
        def _():
            pass_down(layer).wait_recv()
            spread_frames(taps, 0, 0, earlier_above.at[layer])

        @pl.when(has_down)
        def _():
            pass_up(layer).wait_recv()
            spread_frames(taps, 0, 5, earlier_below.at[layer])

    def each_pair(step):
        def body(k, carry):
            step(k, (1 - k, 2 + k))
            return carry

        lax.fori_loop(0, 2, body, 0)

    def cut(part, i, j):
        return part[i * channels : (i + 1) * channels, j * columns : (j + 1) * columns]

    def plus_bias(part, bias):
        wide = jnp.concatenate([bias, bias], axis=1)
        return part + jnp.concatenate([wide, wide], axis=0)

    channels, columns = features.shape[2:]
    two = 2 * channels
    for load in loads[:4]:
        load.wait()
    first_gain, first_bias, second_gain, second_bias = (
        column(vectors, i, columns) for i in range(4)
    )

    def first_activation(rows):
        def step(half, carry):
            for i in range(2):
                f = 2 * half + i
                for r in rows:
                    act = activate(features[f, r].astype(jnp.float32), first_gain)
                    own[0, f, r] = act.astype(jnp.bfloat16)
                    spread(taps_a, f + 2, r + 1, act)
            return carry

        lax.fori_loop(0, 2, step, 0)

    first_activation((0, 3))
    pl.semaphore_wait(
        barrier,
        sum(present.astype(jnp.int32) for present, _ in neighbours),
    )
    send_rows(0, 0)
    send_later(0, (0, 1))
    first_activation((1, 2))
    send_later(0, (2,))

    loads[4].wait()
    stack(weights_a, first_weight)
    clear_edges(taps_a)
    clear_edges(taps_b)

    def second_activation(first, pair, part):
        for i in range(2):
            for j, r in enumerate(pair):
                act = activate(cut(part, i, j), second_gain)
                own[1, first + i, r] = act.astype(jnp.bfloat16)
                spread(taps_b, first + i + 2, r + 1, act)

    def finish(first, pair, part):
        for i in range(2):
            for j, r in enumerate(pair):
                value = features[first + i, r].astype(jnp.float32) + cut(part, i, j)
                out[first + i, r] = value.astype(jnp.bfloat16)

    def first_late(k, pair):
        @pl.when(k == 1)
        def _():
            loads[5].wait()
            stack(weights_b, second_weight)
            take_rows(0, taps_a, 0)

        both = multiply(weights_a[...], taps_a, 2, pair)
        total[0, k] = plus_bias(both[:two, :], first_bias)
        part = both[two:, :] + multiply(weights_a[:two, :], taps_a, 4, pair)
        second_activation(2, pair, plus_bias(part, first_bias))

    each_pair(first_late)
    send_rows(1, 1)

    def second_late(k, pair):
        @pl.when(has_next)
        def _():
            part = multiply(weights_b[...], taps_b, 4, pair)
            total[1, k] = plus_bias(part[:two, :], second_bias)
            for i in range(2):
                for j, r in enumerate(pair):
                    partial[i, r] = cut(part, 2 + i, j).astype(jnp.bfloat16)

        @pl.when(jnp.logical_not(has_next))
        def _():
            part = multiply(weights_b[:two, :], taps_b, 4, pair)
            total[1, k] = plus_bias(part, second_bias)

    second_late(0, (1, 2))
    send_later(1, (2,))

    pass_on(0)
    take_rows(1, taps_b, 1)
    second_late(1, (0, 3))
    send_later(1, (0, 1))

    @pl.when(has_prev)
    def _():
        take_earlier(0, taps_a)

    def first_earlier(k, pair):
        @pl.when(has_prev)
        def _():
            @pl.when(k == 1)
            def _():
                take_corners(0, taps_a)

            total[0, k] += multiply(weights_a[two:, :], taps_a, 0, pair)

        second_activation(0, pair, total[0, k])

    each_pair(first_earlier)
    send_rows(1, 0)

    def second_early(k, pair):
        @pl.when(k == 1)
        def _():
            take_rows(1, taps_b, 0)

        part = multiply(weights_b[...], taps_b, 2, pair)
        finish(2, pair, total[1, k] + part[two:, :])
        total[0, k] = plus_bias(part[:two, :], second_bias)

        @pl.when(has_prev)
        def _():
            @pl.when(k == 0)
            def _():
                to_later(1, 2).wait_recv()

            @pl.when(k == 1)
            def _():
                to_later(1, 0).wait_recv()
                to_later(1, 1).wait_recv()

            for i in range(2):
                for j, r in enumerate(pair):
                    block = (
                        pl.ds(i * channels, channels),
                        pl.ds(j * columns, columns),
                    )
                    total[0, k, *block] += earlier[1, i, r].astype(jnp.float32)

        finish(0, pair, total[0, k])

    each_pair(second_early)

    for layer in range(2):

        @pl.when(has_up)
        def _():
            for half in halves(layer):
                to_up(layer, half).wait_send()

        @pl.when(has_down)
        def _():
            for half in halves(layer):
                to_down(layer, half).wait_send()

        @pl.when(has_next)
        def _():
            for part in range(3):
                to_later(layer, part).wait_send()

    @pl.when(has_prev & has_up)
    def _():
        pass_up(0).wait_send()

    @pl.when(has_prev & has_down)
    def _():
        pass_down(0).wait_send()


def local(features, first_gain, first_weight, first_bias, second_gain, second_weight, second_bias):
    channels, frames, rows, columns = features.shape
    by_row = jnp.transpose(features, (1, 2, 0, 3))
    vectors = [v.reshape(1, channels) for v in (first_gain, first_bias, second_gain, second_bias)]
    vmem = pl.BlockSpec(memory_space=pltpu.VMEM)
    act = jnp.bfloat16
    stacked = (4 * channels, 2 * padded_width(first_weight.shape[1] // 3))
    cells = 2 * channels * first_weight.shape[1] * frames * rows * columns
    result = pl.pallas_call(
        functools.partial(kernel, lax.axis_size("tm"), lax.axis_size("height")),
        out_shape=jax.ShapeDtypeStruct(by_row.shape, jnp.bfloat16),
        in_specs=[vmem] + [pl.BlockSpec(memory_space=pltpu.HBM)] * 6,
        out_specs=vmem,
        scratch_shapes=[
            pltpu.VMEM((4, 1, channels), jnp.float32),
            pltpu.VMEM(first_weight.shape, act),
            pltpu.VMEM(second_weight.shape, act),
            pltpu.VMEM(stacked, act),
            pltpu.VMEM(stacked, act),
            pltpu.VMEM((2, frames, rows, channels, columns), act),
            pltpu.VMEM((2, frames, channels, columns), act),
            pltpu.VMEM((2, frames, channels, columns), act),
            pltpu.VMEM((2, 2, rows, channels, columns), act),
            pltpu.VMEM((2, 2, channels, columns), act),
            pltpu.VMEM((2, 2, channels, columns), act),
            pltpu.VMEM((2, rows, channels, columns), act),
            pltpu.VMEM((frames + 2, rows + 2, 3, channels, columns), act),
            pltpu.VMEM((frames + 2, rows + 2, 3, channels, columns), act),
            pltpu.VMEM((2, 2, 2 * channels, 2 * columns), jnp.float32),
            pltpu.SemaphoreType.DMA((2, 9)),
            pltpu.SemaphoreType.DMA((2, 9)),
            pltpu.SemaphoreType.DMA((6,)),
        ],
        compiler_params=pltpu.CompilerParams(
            collective_id=0, has_side_effects=True, vmem_limit_bytes=53 * 1024 * 1024
        ),
        cost_estimate=pl.CostEstimate(
            flops=2 * cells, bytes_accessed=3 * features.size * 2, transcendentals=features.size * 4
        ),
    )(by_row, first_weight, second_weight, *vectors)
    return jnp.transpose(result, (2, 0, 1, 3))


def solution(mesh):
    return jax.shard_map(
        local,
        mesh=mesh,
        in_specs=(P(None, "tm", "height", None), P(), P(), P(), P(), P(), P()),
        out_specs=P(None, "tm", "height", None),
        check_vma=False,
    )
```

```python
import functools

import jax
import jax.numpy as jnp
from jax import lax
from jax.experimental import pallas as pl
from jax.experimental.pallas import tpu as pltpu
from jax.sharding import PartitionSpec as P

MESH = pl.DeviceIdType.MESH

def activate(values, gain):
    mean_square = jnp.mean(values * values, axis=0, keepdims=True)
    scaled = values * lax.rsqrt(mean_square + 1e-06) * gain
    return scaled * (0.5 + 0.5 * jnp.tanh(0.5 * scaled))


def spread(taps, frame, row, values):
    values = values.astype(jnp.bfloat16)
    lanes = lax.broadcasted_iota(jnp.int32, values.shape, 1)
    last = values.shape[1] - 1
    zero = jnp.zeros_like(values)
    taps[frame, row, 0] = jnp.where(lanes == 0, zero, pltpu.roll(values, 1, 1))
    taps[frame, row, 1] = values
    taps[frame, row, 2] = jnp.where(lanes == last, zero, pltpu.roll(values, last, 1))


def padded_width(width):
    return -(-width // 128) * 128


def window(taps, frame, pair):
    width, columns = 9 * taps.shape[3], taps.shape[4]
    zero = jnp.zeros((padded_width(width) - width, len(pair) * columns), taps.dtype)
    blocks = []
    for i in range(2):
        rows = [taps[frame + i, pl.ds(r, 3)].reshape(width, columns) for r in pair]
        blocks += [jnp.concatenate(rows, axis=1), zero]
    return jnp.concatenate(blocks, axis=0)


def multiply(weights, taps, frame, pair):
    return jnp.dot(weights, window(taps, frame, pair), preferred_element_type=jnp.float32)


def stack(weights, source):
    channels = source.shape[0]
    width = source.shape[1] // 3
    full = padded_width(width)
    zero = jnp.zeros((channels, full - width), source.dtype)
    early, middle, late = (
        jnp.concatenate([source[:, p * width : (p + 1) * width], zero], axis=1) for p in range(3)
    )
    none = jnp.zeros_like(early)
    for i, blocks in enumerate(((late, none), (middle, late), (early, middle), (none, early))):
        for j, block in enumerate(blocks):
            weights[i * channels : (i + 1) * channels, j * full : (j + 1) * full] = block


def column(vectors, i, columns):
    wide = jnp.broadcast_to(vectors[i], (columns, vectors.shape[2]))
    return jnp.transpose(wide)


def kernel(
    tm_count,
    height_count,
    features,
    first_weight_hbm,
    second_weight_hbm,
    first_gain_hbm,
    first_bias_hbm,
    second_gain_hbm,
    second_bias_hbm,
    out,
    vectors,
    first_weight,
    second_weight,
    weights_a,
    weights_b,
    own,
    above,
    below,
    earlier,
    earlier_above,
    earlier_below,
    partial,
    taps_a,
    taps_b,
    total,
    send_sem,
    recv_sem,
    load_sem,
):
    loads = [
        pltpu.make_async_copy(source, target, load_sem.at[i])
        for i, (source, target) in enumerate(
            (
                (first_gain_hbm, vectors.at[0]),
                (first_bias_hbm, vectors.at[1]),
                (second_gain_hbm, vectors.at[2]),
                (second_bias_hbm, vectors.at[3]),
                (first_weight_hbm, first_weight),
                (second_weight_hbm, second_weight),
            )
        )
    ]
    for load in loads:
        load.start()
    t = lax.axis_index("tm")
    h = lax.axis_index("height")
    has_prev, has_next = t > 0, t < tm_count - 1
    has_up, has_down = h > 0, h < height_count - 1
    up, down = (t, h - 1), (t, h + 1)
    later = (t + 1, h)

    barrier = pltpu.get_barrier_semaphore()
    neighbours = (
        (has_prev, (t - 1, h)),
        (has_next, later),
        (has_up, up),
        (has_down, down),
    )
    for present, device in neighbours:

        @pl.when(present)
        def _():
            pl.semaphore_signal(barrier, inc=1, device_id=device, device_id_type=MESH)

    def message(layer, slot, source, target, device):
        return pltpu.make_async_remote_copy(
            src_ref=source,
            dst_ref=target,
            send_sem=send_sem.at[layer, slot],
            recv_sem=recv_sem.at[layer, slot],
            device_id=device,
            device_id_type=MESH,
        )

    def to_up(layer, half):
        frames = pl.ds(2 * half, 2)
        return message(
            layer, half, own.at[layer, frames, 0], below.at[layer, frames], up
        )

    def to_down(layer, half):
        frames = pl.ds(2 * half, 2)
        return message(
            layer, 2 + half, own.at[layer, frames, 3], above.at[layer, frames], down
        )

    def to_later(layer, part):
        row, count = ((0, 1), (3, 1), (1, 2))[part]
        rows = pl.ds(row, count)
        return message(
            layer,
            4 + part,
            partial.at[:, rows] if layer else own.at[layer, pl.ds(2, 2), rows],
            earlier.at[layer, :, rows],
            later,
        )

    def pass_up(layer):
        return message(layer, 7, earlier.at[layer, :, 0], earlier_below.at[layer], up)

    def pass_down(layer):
        return message(layer, 8, earlier.at[layer, :, 3], earlier_above.at[layer], down)

    def send_rows(layer, half):
        @pl.when(has_up)
        def _():
            to_up(layer, half).start()

        @pl.when(has_down)
        def _():
            to_down(layer, half).start()

    def send_later(layer, parts):
        @pl.when(has_next)
        def _():
            for part in parts:
                to_later(layer, part).start()

    def clear(taps, frames, row):
        for frame in frames:
            taps[frame, row] = jnp.zeros(taps.shape[2:], taps.dtype)

    def spread_frames(taps, first, row, source):
        def step(f, carry):
            spread(taps, first + f, row, source[f])
            return carry

        lax.fori_loop(0, 2, step, 0)

    def take_rows(layer, taps, half):
        frames = pl.ds(2 * half, 2)

        @pl.when(has_up)
        def _():
            to_down(layer, half).wait_recv()
            spread_frames(taps, 2 + 2 * half, 0, above.at[layer, frames])

        @pl.when(has_down)
        def _():
            to_up(layer, half).wait_recv()
            spread_frames(taps, 2 + 2 * half, 5, below.at[layer, frames])

    def clear_edges(taps):
        @pl.when(jnp.logical_not(has_up))
        def _():
            clear(taps, range(6), 0)

        @pl.when(jnp.logical_not(has_down))
        def _():
            clear(taps, range(6), 5)

    def pass_on(layer):
        @pl.when(has_prev)
        def _():
            to_later(layer, 0).wait_recv()

            @pl.when(has_up)
            def _():
                pass_up(layer).start()

            to_later(layer, 1).wait_recv()

            @pl.when(has_down)
            def _():
                pass_down(layer).start()

    def take_earlier(layer, taps):
        to_later(layer, 2).wait_recv()

        def step(f, carry):
            for r in range(4):
                spread(taps, f, r + 1, earlier[layer, f, r])
            return carry

        lax.fori_loop(0, 2, step, 0)

    def take_corners(layer, taps):
        @pl.when(has_up)
        def _():
            pass_down(layer).wait_recv()
            spread_frames(taps, 0, 0, earlier_above.at[layer])

        @pl.when(has_down)
        def _():
            pass_up(layer).wait_recv()
            spread_frames(taps, 0, 5, earlier_below.at[layer])

    def each_pair(step):
        def body(k, carry):
            step(k, (1 - k, 2 + k))
            return carry

        lax.fori_loop(0, 2, body, 0)

    def cut(part, i, j):
        return part[i * channels : (i + 1) * channels, j * columns : (j + 1) * columns]

    def plus_bias(part, bias):
        wide = jnp.concatenate([bias, bias], axis=1)
        return part + jnp.concatenate([wide, wide], axis=0)

    channels, columns = features.shape[2:]
    two = 2 * channels
    for load in loads[:4]:
        load.wait()
    first_gain, first_bias, second_gain, second_bias = (
        column(vectors, i, columns) for i in range(4)
    )

    def first_activation(f, carry):
        for r in range(4):
            act = activate(features[f, r].astype(jnp.float32), first_gain)
            own[0, f, r] = act.astype(jnp.bfloat16)
            spread(taps_a, f + 2, r + 1, act)
        return carry

    lax.fori_loop(0, 4, first_activation, 0)

    pl.semaphore_wait(
        barrier,
        sum(present.astype(jnp.int32) for present, _ in neighbours),
    )
    send_rows(0, 1)
    send_rows(0, 0)
    send_later(0, (0, 1, 2))

    loads[4].wait()
    stack(weights_a, first_weight)
    clear_edges(taps_a)
    clear_edges(taps_b)

    def second_activation(first, pair, part):
        for i in range(2):
            for j, r in enumerate(pair):
                act = activate(cut(part, i, j), second_gain)
                own[1, first + i, r] = act.astype(jnp.bfloat16)
                spread(taps_b, first + i + 2, r + 1, act)

    def finish(first, pair, part):
        for i in range(2):
            for j, r in enumerate(pair):
                value = features[first + i, r].astype(jnp.float32) + cut(part, i, j)
                out[first + i, r] = value.astype(jnp.bfloat16)

    def first_late(k, pair):
        @pl.when(k == 1)
        def _():
            loads[5].wait()
            stack(weights_b, second_weight)
            take_rows(0, taps_a, 1)
            take_rows(0, taps_a, 0)

        part = multiply(weights_a[two:, :], taps_a, 2, pair)
        part = part + multiply(weights_a[:two, :], taps_a, 4, pair)
        second_activation(2, pair, plus_bias(part, first_bias))

    each_pair(first_late)
    send_rows(1, 1)

    def second_late(k, pair):
        @pl.when(has_next)
        def _():
            part = multiply(weights_b[...], taps_b, 4, pair)
            total[1, k] = plus_bias(part[:two, :], second_bias)
            for i in range(2):
                for j, r in enumerate(pair):
                    partial[i, r] = cut(part, 2 + i, j).astype(jnp.bfloat16)

        @pl.when(jnp.logical_not(has_next))
        def _():
            part = multiply(weights_b[:two, :], taps_b, 4, pair)
            total[1, k] = plus_bias(part, second_bias)

    second_late(0, (1, 2))
    send_later(1, (2,))

    def first_early(k, pair):
        total[0, k] = plus_bias(multiply(weights_a[:two, :], taps_a, 2, pair), first_bias)

    each_pair(first_early)

    pass_on(0)

    def finish_late():
        take_rows(1, taps_b, 1)
        second_late(1, (0, 3))
        send_later(1, (0, 1))

    between = has_prev & has_next

    @pl.when(between)
    def _():
        finish_late()

    @pl.when(has_prev)
    def _():
        take_earlier(0, taps_a)

    def first_earlier(k, pair):
        @pl.when(has_prev)
        def _():
            @pl.when(k == 1)
            def _():
                take_corners(0, taps_a)

            total[0, k] += multiply(weights_a[two:, :], taps_a, 0, pair)

        second_activation(0, pair, total[0, k])

    each_pair(first_earlier)
    send_rows(1, 0)

    @pl.when(jnp.logical_not(between))
    def _():
        finish_late()

    def second_early(k, pair):
        @pl.when(k == 1)
        def _():
            take_rows(1, taps_b, 0)

        part = multiply(weights_b[...], taps_b, 2, pair)
        finish(2, pair, total[1, k] + part[two:, :])
        total[0, k] = plus_bias(part[:two, :], second_bias)

        @pl.when(has_prev)
        def _():
            @pl.when(k == 0)
            def _():
                to_later(1, 2).wait_recv()

            @pl.when(k == 1)
            def _():
                to_later(1, 0).wait_recv()
                to_later(1, 1).wait_recv()

            for i in range(2):
                for j, r in enumerate(pair):
                    block = (
                        pl.ds(i * channels, channels),
                        pl.ds(j * columns, columns),
                    )
                    total[0, k, *block] += earlier[1, i, r].astype(jnp.float32)

        finish(0, pair, total[0, k])

    each_pair(second_early)

    for layer in range(2):

        @pl.when(has_up)
        def _():
            for half in range(2):
                to_up(layer, half).wait_send()

        @pl.when(has_down)
        def _():
            for half in range(2):
                to_down(layer, half).wait_send()

        @pl.when(has_next)
        def _():
            for part in range(3):
                to_later(layer, part).wait_send()

    @pl.when(has_prev & has_up)
    def _():
        pass_up(0).wait_send()

    @pl.when(has_prev & has_down)
    def _():
        pass_down(0).wait_send()


def local(features, first_gain, first_weight, first_bias, second_gain, second_weight, second_bias):
    channels, frames, rows, columns = features.shape
    by_row = jnp.transpose(features, (1, 2, 0, 3))
    vectors = [v.reshape(1, channels) for v in (first_gain, first_bias, second_gain, second_bias)]
    vmem = pl.BlockSpec(memory_space=pltpu.VMEM)
    act = jnp.bfloat16
    stacked = (4 * channels, 2 * padded_width(first_weight.shape[1] // 3))
    cells = 2 * channels * first_weight.shape[1] * frames * rows * columns
    result = pl.pallas_call(
        functools.partial(kernel, lax.axis_size("tm"), lax.axis_size("height")),
        out_shape=jax.ShapeDtypeStruct(by_row.shape, jnp.bfloat16),
        in_specs=[vmem] + [pl.BlockSpec(memory_space=pltpu.HBM)] * 6,
        out_specs=vmem,
        scratch_shapes=[
            pltpu.VMEM((4, 1, channels), jnp.float32),
            pltpu.VMEM(first_weight.shape, act),
            pltpu.VMEM(second_weight.shape, act),
            pltpu.VMEM(stacked, act),
            pltpu.VMEM(stacked, act),
            pltpu.VMEM((2, frames, rows, channels, columns), act),
            pltpu.VMEM((2, frames, channels, columns), act),
            pltpu.VMEM((2, frames, channels, columns), act),
            pltpu.VMEM((2, 2, rows, channels, columns), act),
            pltpu.VMEM((2, 2, channels, columns), act),
            pltpu.VMEM((2, 2, channels, columns), act),
            pltpu.VMEM((2, rows, channels, columns), act),
            pltpu.VMEM((frames + 2, rows + 2, 3, channels, columns), act),
            pltpu.VMEM((frames + 2, rows + 2, 3, channels, columns), act),
            pltpu.VMEM((2, 2, 2 * channels, 2 * columns), jnp.float32),
            pltpu.SemaphoreType.DMA((2, 9)),
            pltpu.SemaphoreType.DMA((2, 9)),
            pltpu.SemaphoreType.DMA((6,)),
        ],
        compiler_params=pltpu.CompilerParams(
            collective_id=0, has_side_effects=True, vmem_limit_bytes=53 * 1024 * 1024
        ),
        cost_estimate=pl.CostEstimate(
            flops=2 * cells, bytes_accessed=3 * features.size * 2, transcendentals=features.size * 4
        ),
    )(by_row, first_weight, second_weight, *vectors)
    return jnp.transpose(result, (2, 0, 1, 3))


def solution(mesh):
    return jax.shard_map(
        local,
        mesh=mesh,
        in_specs=(P(None, "tm", "height", None), P(), P(), P(), P(), P(), P()),
        out_specs=P(None, "tm", "height", None),
        check_vma=False,
    )
```

```python
import functools

import jax
import jax.numpy as jnp
from jax import lax
from jax.experimental import pallas as pl
from jax.experimental.pallas import tpu as pltpu
from jax.sharding import PartitionSpec as P

MESH = pl.DeviceIdType.MESH

def activate(values, gain):
    mean_square = jnp.mean(values * values, axis=0, keepdims=True)
    scaled = values * lax.rsqrt(mean_square + 1e-06) * gain
    return scaled * (0.5 + 0.5 * jnp.tanh(0.5 * scaled))


def spread(taps, frame, row, values):
    values = values.astype(jnp.bfloat16)
    lanes = lax.broadcasted_iota(jnp.int32, values.shape, 1)
    last = values.shape[1] - 1
    zero = jnp.zeros_like(values)
    taps[frame, row, 0] = jnp.where(lanes == 0, zero, pltpu.roll(values, 1, 1))
    taps[frame, row, 1] = values
    taps[frame, row, 2] = jnp.where(lanes == last, zero, pltpu.roll(values, last, 1))


def padded_width(width):
    return -(-width // 128) * 128


def window(taps, frame, pair):
    width, columns = 9 * taps.shape[3], taps.shape[4]
    zero = jnp.zeros((padded_width(width) - width, len(pair) * columns), taps.dtype)
    blocks = []
    for i in range(2):
        rows = [taps[frame + i, pl.ds(r, 3)].reshape(width, columns) for r in pair]
        blocks += [jnp.concatenate(rows, axis=1), zero]
    return jnp.concatenate(blocks, axis=0)


def multiply(weights, taps, frame, pair):
    return jnp.dot(weights, window(taps, frame, pair), preferred_element_type=jnp.float32)


def stack(weights, source):
    channels = source.shape[0]
    width = source.shape[1] // 3
    full = padded_width(width)
    zero = jnp.zeros((channels, full - width), source.dtype)
    early, middle, late = (
        jnp.concatenate([source[:, p * width : (p + 1) * width], zero], axis=1) for p in range(3)
    )
    none = jnp.zeros_like(early)
    for i, blocks in enumerate(((late, none), (middle, late), (early, middle), (none, early))):
        for j, block in enumerate(blocks):
            weights[i * channels : (i + 1) * channels, j * full : (j + 1) * full] = block


def column(vectors, i, columns):
    wide = jnp.broadcast_to(vectors[i], (columns, vectors.shape[2]))
    return jnp.transpose(wide)


def kernel(
    tm_count,
    height_count,
    features,
    first_weight_hbm,
    second_weight_hbm,
    first_gain_hbm,
    first_bias_hbm,
    second_gain_hbm,
    second_bias_hbm,
    out,
    vectors,
    first_weight,
    second_weight,
    weights_a,
    weights_b,
    own,
    above,
    below,
    earlier,
    earlier_above,
    earlier_below,
    partial,
    taps_a,
    taps_b,
    total,
    send_sem,
    recv_sem,
    load_sem,
):
    loads = [
        pltpu.make_async_copy(source, target, load_sem.at[i])
        for i, (source, target) in enumerate(
            (
                (first_gain_hbm, vectors.at[0]),
                (first_bias_hbm, vectors.at[1]),
                (second_gain_hbm, vectors.at[2]),
                (second_bias_hbm, vectors.at[3]),
                (first_weight_hbm, first_weight),
                (second_weight_hbm, second_weight),
            )
        )
    ]
    for load in loads:
        load.start()
    t = lax.axis_index("tm")
    h = lax.axis_index("height")
    has_prev, has_next = t > 0, t < tm_count - 1
    has_up, has_down = h > 0, h < height_count - 1
    up, down = (t, h - 1), (t, h + 1)
    later = (t + 1, h)

    barrier = pltpu.get_barrier_semaphore()
    neighbours = (
        (has_prev, (t - 1, h)),
        (has_next, later),
        (has_up, up),
        (has_down, down),
    )
    for present, device in neighbours:

        @pl.when(present)
        def _():
            pl.semaphore_signal(barrier, inc=1, device_id=device, device_id_type=MESH)

    def message(layer, slot, source, target, device):
        return pltpu.make_async_remote_copy(
            src_ref=source,
            dst_ref=target,
            send_sem=send_sem.at[layer, slot],
            recv_sem=recv_sem.at[layer, slot],
            device_id=device,
            device_id_type=MESH,
        )

    def to_up(layer, half):
        frames = pl.ds(2 * half, 2)
        return message(
            layer, half, own.at[layer, frames, 0], below.at[layer, frames], up
        )

    def to_down(layer, half):
        frames = pl.ds(2 * half, 2)
        return message(
            layer, 2 + half, own.at[layer, frames, 3], above.at[layer, frames], down
        )

    def to_later(layer, part):
        row, count = ((0, 1), (3, 1), (1, 2))[part]
        rows = pl.ds(row, count)
        return message(
            layer,
            4 + part,
            partial.at[:, rows] if layer else own.at[layer, pl.ds(2, 2), rows],
            earlier.at[layer, :, rows],
            later,
        )

    def pass_up(layer):
        return message(layer, 7, earlier.at[layer, :, 0], earlier_below.at[layer], up)

    def pass_down(layer):
        return message(layer, 8, earlier.at[layer, :, 3], earlier_above.at[layer], down)

    def send_rows(layer, half):
        @pl.when(has_up)
        def _():
            to_up(layer, half).start()

        @pl.when(has_down)
        def _():
            to_down(layer, half).start()

    def send_later(layer, parts):
        @pl.when(has_next)
        def _():
            for part in parts:
                to_later(layer, part).start()

    def clear(taps, frames, row):
        for frame in frames:
            taps[frame, row] = jnp.zeros(taps.shape[2:], taps.dtype)

    def spread_frames(taps, first, row, source):
        def step(f, carry):
            spread(taps, first + f, row, source[f])
            return carry

        lax.fori_loop(0, 2, step, 0)

    def take_rows(layer, taps, half):
        frames = pl.ds(2 * half, 2)

        @pl.when(has_up)
        def _():
            to_down(layer, half).wait_recv()
            spread_frames(taps, 2 + 2 * half, 0, above.at[layer, frames])

        @pl.when(has_down)
        def _():
            to_up(layer, half).wait_recv()
            spread_frames(taps, 2 + 2 * half, 5, below.at[layer, frames])

    def clear_edges(taps):
        @pl.when(jnp.logical_not(has_up))
        def _():
            clear(taps, range(6), 0)

        @pl.when(jnp.logical_not(has_down))
        def _():
            clear(taps, range(6), 5)

    def pass_on(layer):
        @pl.when(has_prev)
        def _():
            to_later(layer, 0).wait_recv()

            @pl.when(has_up)
            def _():
                pass_up(layer).start()

            to_later(layer, 1).wait_recv()

            @pl.when(has_down)
            def _():
                pass_down(layer).start()

    def take_earlier(layer, taps):
        to_later(layer, 2).wait_recv()

        def step(f, carry):
            for r in range(4):
                spread(taps, f, r + 1, earlier[layer, f, r])
            return carry

        lax.fori_loop(0, 2, step, 0)

    def take_corners(layer, taps):
        @pl.when(has_up)
        def _():
            pass_down(layer).wait_recv()
            spread_frames(taps, 0, 0, earlier_above.at[layer])

        @pl.when(has_down)
        def _():
            pass_up(layer).wait_recv()
            spread_frames(taps, 0, 5, earlier_below.at[layer])

    def each_pair(step):
        def body(k, carry):
            step(k, (1 - k, 2 + k))
            return carry

        lax.fori_loop(0, 2, body, 0)

    def cut(part, i, j):
        return part[i * channels : (i + 1) * channels, j * columns : (j + 1) * columns]

    def plus_bias(part, bias):
        wide = jnp.concatenate([bias, bias], axis=1)
        return part + jnp.concatenate([wide, wide], axis=0)

    channels, columns = features.shape[2:]
    two = 2 * channels
    for load in loads[:4]:
        load.wait()
    first_gain, first_bias, second_gain, second_bias = (
        column(vectors, i, columns) for i in range(4)
    )

    def first_activation(f, carry):
        for r in range(4):
            act = activate(features[f, r].astype(jnp.float32), first_gain)
            own[0, f, r] = act.astype(jnp.bfloat16)
            spread(taps_a, f + 2, r + 1, act)
        return carry

    lax.fori_loop(0, 4, first_activation, 0)

    pl.semaphore_wait(
        barrier,
        sum(present.astype(jnp.int32) for present, _ in neighbours),
    )
    send_rows(0, 1)
    send_rows(0, 0)
    send_later(0, (0, 1, 2))

    loads[4].wait()
    stack(weights_a, first_weight)
    clear_edges(taps_a)
    clear_edges(taps_b)

    def second_activation(first, pair, part):
        for i in range(2):
            for j, r in enumerate(pair):
                act = activate(cut(part, i, j), second_gain)
                own[1, first + i, r] = act.astype(jnp.bfloat16)
                spread(taps_b, first + i + 2, r + 1, act)

    def finish(first, pair, part):
        for i in range(2):
            for j, r in enumerate(pair):
                value = features[first + i, r].astype(jnp.float32) + cut(part, i, j)
                out[first + i, r] = value.astype(jnp.bfloat16)

    def first_late(k, pair):
        @pl.when(k == 1)
        def _():
            loads[5].wait()
            stack(weights_b, second_weight)
            take_rows(0, taps_a, 1)
            take_rows(0, taps_a, 0)

        part = multiply(weights_a[two:, :], taps_a, 2, pair)
        part = part + multiply(weights_a[:two, :], taps_a, 4, pair)
        second_activation(2, pair, plus_bias(part, first_bias))

    each_pair(first_late)
    send_rows(1, 1)

    def second_late(k, pair):
        @pl.when(has_next)
        def _():
            part = multiply(weights_b[...], taps_b, 4, pair)
            total[1, k] = plus_bias(part[:two, :], second_bias)
            for i in range(2):
                for j, r in enumerate(pair):
                    partial[i, r] = cut(part, 2 + i, j).astype(jnp.bfloat16)

        @pl.when(jnp.logical_not(has_next))
        def _():
            part = multiply(weights_b[:two, :], taps_b, 4, pair)
            total[1, k] = plus_bias(part, second_bias)

    second_late(0, (1, 2))
    send_later(1, (2,))

    pass_on(0)

    def first_early(k, pair):
        total[0, k] = plus_bias(multiply(weights_a[:two, :], taps_a, 2, pair), first_bias)

    each_pair(first_early)


    def finish_late():
        take_rows(1, taps_b, 1)
        second_late(1, (0, 3))
        send_later(1, (0, 1))

    between = has_prev & has_next

    @pl.when(between)
    def _():
        finish_late()

    @pl.when(has_prev)
    def _():
        take_earlier(0, taps_a)

    def first_earlier(k, pair):
        @pl.when(has_prev)
        def _():
            @pl.when(k == 1)
            def _():
                take_corners(0, taps_a)

            total[0, k] += multiply(weights_a[two:, :], taps_a, 0, pair)

        second_activation(0, pair, total[0, k])

    each_pair(first_earlier)
    send_rows(1, 0)

    @pl.when(jnp.logical_not(between))
    def _():
        finish_late()

    def second_early(k, pair):
        @pl.when(k == 1)
        def _():
            take_rows(1, taps_b, 0)

        part = multiply(weights_b[...], taps_b, 2, pair)
        finish(2, pair, total[1, k] + part[two:, :])
        total[0, k] = plus_bias(part[:two, :], second_bias)

        @pl.when(has_prev)
        def _():
            @pl.when(k == 0)
            def _():
                to_later(1, 2).wait_recv()

            @pl.when(k == 1)
            def _():
                to_later(1, 0).wait_recv()
                to_later(1, 1).wait_recv()

            for i in range(2):
                for j, r in enumerate(pair):
                    block = (
                        pl.ds(i * channels, channels),
                        pl.ds(j * columns, columns),
                    )
                    total[0, k, *block] += earlier[1, i, r].astype(jnp.float32)

        finish(0, pair, total[0, k])

    each_pair(second_early)

    for layer in range(2):

        @pl.when(has_up)
        def _():
            for half in range(2):
                to_up(layer, half).wait_send()

        @pl.when(has_down)
        def _():
            for half in range(2):
                to_down(layer, half).wait_send()

        @pl.when(has_next)
        def _():
            for part in range(3):
                to_later(layer, part).wait_send()

    @pl.when(has_prev & has_up)
    def _():
        pass_up(0).wait_send()

    @pl.when(has_prev & has_down)
    def _():
        pass_down(0).wait_send()


def local(features, first_gain, first_weight, first_bias, second_gain, second_weight, second_bias):
    channels, frames, rows, columns = features.shape
    by_row = jnp.transpose(features, (1, 2, 0, 3))
    vectors = [v.reshape(1, channels) for v in (first_gain, first_bias, second_gain, second_bias)]
    vmem = pl.BlockSpec(memory_space=pltpu.VMEM)
    act = jnp.bfloat16
    stacked = (4 * channels, 2 * padded_width(first_weight.shape[1] // 3))
    cells = 2 * channels * first_weight.shape[1] * frames * rows * columns
    result = pl.pallas_call(
        functools.partial(kernel, lax.axis_size("tm"), lax.axis_size("height")),
        out_shape=jax.ShapeDtypeStruct(by_row.shape, jnp.bfloat16),
        in_specs=[vmem] + [pl.BlockSpec(memory_space=pltpu.HBM)] * 6,
        out_specs=vmem,
        scratch_shapes=[
            pltpu.VMEM((4, 1, channels), jnp.float32),
            pltpu.VMEM(first_weight.shape, act),
            pltpu.VMEM(second_weight.shape, act),
            pltpu.VMEM(stacked, act),
            pltpu.VMEM(stacked, act),
            pltpu.VMEM((2, frames, rows, channels, columns), act),
            pltpu.VMEM((2, frames, channels, columns), act),
            pltpu.VMEM((2, frames, channels, columns), act),
            pltpu.VMEM((2, 2, rows, channels, columns), act),
            pltpu.VMEM((2, 2, channels, columns), act),
            pltpu.VMEM((2, 2, channels, columns), act),
            pltpu.VMEM((2, rows, channels, columns), act),
            pltpu.VMEM((frames + 2, rows + 2, 3, channels, columns), act),
            pltpu.VMEM((frames + 2, rows + 2, 3, channels, columns), act),
            pltpu.VMEM((2, 2, 2 * channels, 2 * columns), jnp.float32),
            pltpu.SemaphoreType.DMA((2, 9)),
            pltpu.SemaphoreType.DMA((2, 9)),
            pltpu.SemaphoreType.DMA((6,)),
        ],
        compiler_params=pltpu.CompilerParams(
            collective_id=0, has_side_effects=True, vmem_limit_bytes=53 * 1024 * 1024
        ),
        cost_estimate=pl.CostEstimate(
            flops=2 * cells, bytes_accessed=3 * features.size * 2, transcendentals=features.size * 4
        ),
    )(by_row, first_weight, second_weight, *vectors)
    return jnp.transpose(result, (2, 0, 1, 3))


def solution(mesh):
    return jax.shard_map(
        local,
        mesh=mesh,
        in_specs=(P(None, "tm", "height", None), P(), P(), P(), P(), P(), P()),
        out_specs=P(None, "tm", "height", None),
        check_vma=False,
    )
```
